1024 devices in a mesh: grp: 8 (over y), dev: 128 (over x, z, core).
Axes of the slice: x: 4, y: 8, z: 16, core: 2. Of those that a mesh axis runs over, the one named last changes fastest.
Arguments:
- gcm_state: float32 [2048, 3, 1152], P(('grp', 'dev')), may hold values from -6 to 6
- element_op: float32 [2048, 16, 16], P(('grp', 'dev')), may hold values from -1.5 to 1.5
- neighbours: int32 [2048, 4], P(('grp', 'dev')), may hold values from 0 to 2047, as said below
- crm_state: bfloat16 [40960, 2, 3712], P(('grp', 'dev')), may hold values from -6 to 6
- assignment: int32 [32768], P(('grp', 'dev')), may hold values from 0 to 5119, as said below
- column_cost: int32 [32768], P(('grp', 'dev')), may hold values from 1 to 4
Outputs:
- gcm_out: float32 [2048, 3, 1152], P(('grp', 'dev'))
- crm_out: bfloat16 [40960, 2, 3712], P(('grp', 'dev'))
The draws below stay inside these ranges and needn't reach their ends.
Inputs may be any that keep to these rules, and one draw needn't show every extreme that they name: Entry [e, d] is the element across edge d of element e (0 east, 1 north, 2 west, 3 south); that element's edge (d + 2) % 4 meets it point for point in the same order. East and west neighbours lie in e's own block of 2 elements (rows e // 2), north ones in the next block and south ones in the previous block, cyclically over all blocks; the north neighbour of the east neighbour is the east neighbour of the north neighbour, and likewise at every corner. `assignment`: column c belongs to the group of 128 devices along dev that holds it; its value v names device v // 40 of that group and slot v % 40 there. No two columns of a group share a slot; columns go in pairs, so each device sends an even number of columns to each device; each device sends at most 2 columns to one device, some device sends exactly 2 to one, and some device's 40 slots are all filled.
All inputs are finite; a program needn't handle non-finite values.
Results may differ from the reference program's by a relative error of at most 0.0034.
Values may be sent and summed in bfloat16 or wider, within the bound.
A program may use at most 32 MiB of HBM per device.

```python
import jax
import jax.numpy as jnp
from jax import lax

NLEV = 72
CZ = 58
CX = 64
NFIELD = 3
NSUB = 4
NDYN = 3
E_DEV = 2
COLS = 32
DU = 4
PS = 40
ELEMS = 2048
NCOL = 32768
SLOTS = 40960
N_GRP = 8
N_DEV = 128


def draw_neighbours(key, part):
    key = jax.random.fold_in(key, 11)
    row_total = ELEMS // E_DEV
    row_keys = jax.random.split(key, row_total)
    places = jax.vmap(lambda single: jax.random.permutation(single, E_DEV))(row_keys).astype(jnp.int32)
    row_ids = jnp.arange(row_total, dtype=jnp.int32)[:, None]
    cell_ids = jnp.arange(E_DEV, dtype=jnp.int32)[None, :]

    def identity_of(row_value, cell_value):
        row_wrapped = row_value % row_total
        cell_wrapped = cell_value % E_DEV
        return row_wrapped * E_DEV + places[row_wrapped, cell_wrapped]
    east_side = identity_of(row_ids, cell_ids + 1)
    north_side = identity_of(row_ids + 1, cell_ids)
    west_side = identity_of(row_ids, cell_ids - 1)
    south_side = identity_of(row_ids - 1, cell_ids)
    table = jnp.stack([east_side, north_side, west_side, south_side], axis=-1).reshape(-1, 4)
    owners = identity_of(row_ids, cell_ids).reshape(-1)
    return jnp.zeros((ELEMS, 4), jnp.int32).at[owners].set(table)


def draw_assignment(key, part):
    key = jax.random.fold_in(key, 23)
    units = COLS // 2
    half_round = N_DEV // 2
    full_length = (units - DU) * N_DEV
    spots = jnp.arange(units * N_DEV, dtype=jnp.int32)
    in_full = spots < full_length
    remains = jnp.maximum(spots - full_length, 0)
    rounds = jnp.where(in_full, spots // N_DEV, units - DU + remains // half_round)
    places = jnp.where(in_full, spots % N_DEV, remains % half_round)

    def one_group(group_key):
        key_order, key_owner, key_offset, key_columns = jax.random.split(group_key, 4)
        dest_order = jax.random.permutation(key_order, N_DEV).astype(jnp.int32)
        owner_order = jax.random.permutation(key_owner, N_DEV).astype(jnp.int32)
        offsets = jax.random.randint(key_offset, (N_DEV,), 0, PS // 2).astype(jnp.int32)
        column_orders = jax.vmap(lambda single: jax.random.permutation(single, COLS))(jax.random.split(key_columns, N_DEV)).astype(jnp.int32)
        targets = dest_order[places]
        first_slot = (2 * rounds + 2 * offsets[targets]) % PS
        sources = owner_order[spots // units]
        within = spots % units
        first_column = column_orders[sources, 2 * within]
        second_column = column_orders[sources, 2 * within + 1]
        values = jnp.zeros((N_DEV * COLS,), jnp.int32)
        values = values.at[sources * COLS + first_column].set(targets * PS + first_slot)
        values = values.at[sources * COLS + second_column].set(targets * PS + first_slot + 1)
        return values
    groups = jax.vmap(one_group)(jax.random.split(key, N_GRP))
    return groups.reshape(-1)


def place_ends(values, key, low, largest):
    longest = values.shape.index(max(values.shape))
    spots = []
    for shift in (0, 1):
        where = [jax.random.randint(jax.random.fold_in(key, axis), (), 0, length) for axis, length in enumerate(values.shape)]
        where[longest] = (where[longest] + shift) % values.shape[longest]
        spots.append(tuple(where))
    return values.at[spots[0]].set(low).at[spots[1]].set(largest)


def block_levels(rng, shape, cuts, low, largest):
    loudness = 1.0
    for axis_at, blocks in cuts:
        steps = jax.random.uniform(jax.random.fold_in(jax.random.fold_in(rng, 6), axis_at), (blocks,), jnp.float32, low / len(cuts), largest / len(cuts))
        loudness = loudness * jnp.repeat(jnp.exp(steps), shape[axis_at] // blocks).reshape((-1,) + (1,) * (len(shape) - 1 - axis_at))
    return loudness


def normal_values(key, shape, spread, reach, cuts=(), kind=jnp.bfloat16):
    gain = block_levels(key, shape, cuts, -0.22, 0.18) if cuts else 1.0
    values = jax.random.normal(key, shape, jnp.float32) * spread * gain
    return jnp.minimum(jnp.maximum(values, -reach), reach).astype(kind)


def setup_inputs(seed: int = 0) -> dict:
    arg_keys = jax.random.split(jax.random.key(seed), 7)
    return {
        "gcm_state": normal_values(arg_keys[0], (ELEMS, NFIELD, 16 * NLEV), 1.0, 6.0, ((0, 1024),), jnp.float32),
        "element_op": normal_values(arg_keys[1], (ELEMS, 16, 16), 16 ** -0.5, 1.5, ((0, 1024),), jnp.float32),
        "neighbours": draw_neighbours(jax.random.fold_in(arg_keys[6], 71), 0),
        "crm_state": normal_values(arg_keys[3], (SLOTS, 2, CZ * CX), 1.0, 6.0, ((0, 1024),)),
        "assignment": draw_assignment(jax.random.fold_in(arg_keys[6], 71), 0),
        "column_cost": place_ends(jax.random.randint(arg_keys[5], (NCOL,), 1, 5), jax.random.fold_in(arg_keys[5], 1), 1, 4).astype(jnp.int32),
    }


RELAX_RATE = 0.3
HORIZONTAL_MIX = 0.2
VERTICAL_MIX = 0.2
CONDENSE_RATE = 0.5
SATURATION_SLOPE = 0.2
UPPER_DAMPING = 0.5
DYNAMICS_STEP = 0.5


def saturation(temper):
    levels = jnp.arange(CZ, dtype=jnp.float32) / CZ
    return 0.5 - 0.8 * levels[None, :, None] + SATURATION_SLOPE * temper


def cloud_model(crm_in, forcing, step_counts, occupied):
    blocks = crm_in.shape[0]
    fields = crm_in.astype(jnp.float32).reshape(blocks, 2, CZ, CX)
    start_mean = jnp.mean(fields, axis=-1)
    forcing_drive = RELAX_RATE * (forcing[:, 0:2, :CZ] - start_mean)
    for substep in range(NSUB):
        across = jnp.roll(fields, 1, axis=-1) + jnp.roll(fields, -1, axis=-1) - 2.0 * fields
        upward = jnp.concatenate([fields[:, :, 1:], fields[:, :, -1:]], axis=2)
        downward = jnp.concatenate([fields[:, :, :1], fields[:, :, :-1]], axis=2)
        vertical = upward + downward - 2.0 * fields
        stepped = fields + forcing_drive[..., None] + HORIZONTAL_MIX * across + VERTICAL_MIX * vertical
        excess = jax.nn.relu(stepped[:, 1] - saturation(stepped[:, 0]))
        stepped = stepped + jnp.stack([CONDENSE_RATE * excess, -CONDENSE_RATE * excess], axis=1)
        active = (substep < step_counts)[:, None, None, None]
        fields = jnp.where(active, stepped, fields)
    end_mean = jnp.mean(fields, axis=-1)
    cloud_water = jnp.mean(jax.nn.relu(fields[:, 1] - saturation(fields[:, 0])), axis=-1)
    lower_tend = jnp.concatenate([end_mean - start_mean, (cloud_water - forcing[:, 2, :CZ])[:, None]], axis=1)
    occupied_mask = (occupied > 0.5)[:, None, None]
    new_state = jnp.where(occupied_mask, fields.reshape(blocks, 2, CZ * CX).astype(jnp.bfloat16), crm_in)
    return lower_tend, new_state


def assemble(point_grid, north_row, south_row, east_col, west_col, corner_ne, corner_nw, corner_se, corner_sw):
    combined = point_grid.at[:, :, 3].add(north_row)
    combined = combined.at[:, :, 0].add(south_row)
    combined = combined.at[:, :, :, 3].add(east_col)
    combined = combined.at[:, :, :, 0].add(west_col)
    combined = combined.at[:, :, 3, 3].add(corner_ne)
    combined = combined.at[:, :, 3, 0].add(corner_nw)
    combined = combined.at[:, :, 0, 3].add(corner_se)
    combined = combined.at[:, :, 0, 0].add(corner_sw)
    multiplicity = jnp.array([2.0, 1.0, 1.0, 2.0], dtype=jnp.float32)
    weight = 1.0 / (multiplicity[:, None] * multiplicity[None, :])
    return combined * weight[None, None, :, :, None]


def reference(gcm_state, element_op, neighbours, crm_state, assignment, column_cost):
    elements = gcm_state.shape[0]
    total_columns = elements * 16
    state_round = gcm_state.astype(jnp.bfloat16)
    columns = state_round.reshape(elements, 3, 16, NLEV).transpose(0, 2, 1, 3).reshape(total_columns, 3, NLEV)
    group_ids = jnp.arange(total_columns, dtype=jnp.int32) // (N_DEV * COLS)
    slots = group_ids * (N_DEV * PS) + assignment
    total_slots = crm_state.shape[0]
    forcing = jnp.zeros((total_slots, 3, NLEV), jnp.float32).at[slots].set(columns.astype(jnp.float32))
    occupied = jnp.zeros((total_slots,), jnp.float32).at[slots].set(1.0)
    step_counts = jnp.zeros((total_slots,), jnp.int32).at[slots].set(column_cost)
    devices_total = total_slots // PS

    def per_block(pieces):
        crm_block, forcing_block, count_block, occupied_block = pieces
        lower_tend, new_block = cloud_model(crm_block, forcing_block, count_block, occupied_block)
        slot_tend = jnp.concatenate([lower_tend, -UPPER_DAMPING * forcing_block[:, :, CZ:]], axis=2).astype(jnp.bfloat16)
        return slot_tend, new_block

    slot_tends, crm_out = lax.map(per_block, (crm_state.reshape(devices_total, PS, 2, CZ * CX), forcing.reshape(devices_total, PS, 3, NLEV), step_counts.reshape(devices_total, PS), occupied.reshape(devices_total, PS)))
    col_tend = slot_tends.reshape(total_slots, 3, NLEV)[slots].astype(jnp.float32)

    east_ids = neighbours[:, 0]
    north_ids = neighbours[:, 1]
    west_ids = neighbours[:, 2]
    south_ids = neighbours[:, 3]
    dynamic = gcm_state
    for update_index in range(NDYN):
        tendency = jnp.einsum("epq,efqk->efpk", element_op, dynamic.reshape(elements, 3, 16, NLEV), precision=lax.Precision.HIGHEST)
        point_grid = tendency.reshape(elements, 3, 4, 4, NLEV)
        summed = assemble(point_grid, point_grid[north_ids][:, :, 0], point_grid[south_ids][:, :, 3], point_grid[east_ids][:, :, :, 0], point_grid[west_ids][:, :, :, 3], point_grid[north_ids[east_ids]][:, :, 0, 0], point_grid[north_ids[west_ids]][:, :, 0, 3], point_grid[south_ids[east_ids]][:, :, 3, 0], point_grid[south_ids[west_ids]][:, :, 3, 3])
        dynamic = dynamic + DYNAMICS_STEP * summed.reshape(dynamic.shape)
    tend_grid = col_tend.reshape(elements, 16, 3, NLEV).transpose(0, 2, 1, 3).reshape(gcm_state.shape)
    return dynamic + tend_grid, crm_out.reshape(crm_state.shape)
```

```python
import functools

import jax
import jax.numpy as jnp
from jax import lax
from jax.experimental import pallas as pl
from jax.experimental.pallas import tpu as pltpu
from jax.sharding import PartitionSpec as P

NLEV = 72
CZ = 58
CX = 64
HALF = CZ // 2
NSUB = 4
NDYN = 3
COLS = 32
SLOTS = 40
LANES = 128
WIDE = HALF * LANES

MESH = pl.DeviceIdType.MESH
BF16 = jnp.bfloat16
F32 = jnp.float32

LANE_TARGET = 58
LANE_SLOT = 59
LANE_COST = 60


def iota(shape, axis):
    return lax.broadcasted_iota(jnp.int32, shape, axis)


def one_hot(mask, scale=1.0):
    return jnp.where(mask, scale, 0.0).astype(BF16)


def dot(a, b):
    return jnp.dot(a, b, preferred_element_type=F32)


def dot_nt(a, b):
    return lax.dot_general(a, b, (((1,), (1,)), ((), ())), preferred_element_type=F32)


def dot_full(a, b):
    return jnp.dot(a, b, precision=lax.Precision.HIGHEST, preferred_element_type=F32)


def edge_weights(nb_ref):
    shape = (COLS, 48)
    row, col = iota(shape, 0), iota(shape, 1)
    e, p = row // 16, row % 16
    j, i = p // 4, p % 4

    def pick(direction, which):
        first, second = nb_ref[0, direction] % 2, nb_ref[1, direction] % 2
        return jnp.where(which == 0, first, second)

    east, north, west, south = (pick(d, e) for d in range(4))
    side = jnp.where(i == 3, east, west)
    across = 3 - i
    inner = (i == 1) | (i == 2)
    upper, lower = j == 3, j == 0
    count = jnp.where(col == row, 1.0, 0.0)
    add = lambda total, mask: total + jnp.where(mask, 1.0, 0.0)
    count = add(count, ~inner & (col == side * 16 + j * 4 + across))
    count = add(count, upper & (col == 32 + north * 4 + i))
    count = add(count, lower & (col == 40 + south * 4 + i))
    count = add(count, upper & ~inner & (col == 32 + pick(1, side) * 4 + across))
    count = add(count, lower & ~inner & (col == 40 + pick(3, side) * 4 + across))
    share = jnp.where(inner, 1.0, 0.5) * jnp.where(upper | lower, 0.5, 1.0)
    return count * share * 0.5


def kernel(
    dims,
    gcm_ref,
    op_ref,
    nb_ref,
    crm_ref,
    asg_ref,
    cost_ref,
    gout_ref,
    cout_ref,
    dyn,
    base,
    near,
    edge_out,
    edge_in,
    got1,
    pack2,
    got2,
    pack3,
    got3,
    pack4,
    got4,
    state_a,
    state_b,
    drive,
    half_in,
    spread,
    tend,
    s1,
    r1,
    s2,
    r2,
    s3,
    r3,
    s4,
    r4,
    se,
    re,
):
    n_grp, nx, nz, cap = dims
    n_near = nx * 2
    n_dev = n_near * nz
    rows1 = n_near * COLS
    cap2 = cap * n_near
    rows2 = nz * cap2
    grp, dev = lax.axis_index("grp"), lax.axis_index("dev")
    core = dev % 2
    z = (dev // 2) % nz
    x = dev // (2 * nz)
    me = x * 2 + core
    flat = grp * n_dev + dev
    total = n_grp * n_dev

    def flat_device(index):
        return (index // n_dev, index % n_dev)

    north_id = flat_device((flat + 1) % total)
    south_id = flat_device((flat + total - 1) % total)

    def near_device(k):
        return (grp, ((k // 2) * nz + z) * 2 + k % 2)

    def far_device(k):
        return (grp, (x * nz + k) * 2 + core)

    barrier = pltpu.get_barrier_semaphore()
    for o in range(1, n_near):
        pl.semaphore_signal(barrier, 1, device_id=near_device((me + o) % n_near), device_id_type=MESH)
    for o in range(1, nz):
        pl.semaphore_signal(barrier, 1, device_id=far_device((z + o) % nz), device_id_type=MESH)
    pl.semaphore_signal(barrier, 1, device_id=north_id, device_id_type=MESH)
    pl.semaphore_signal(barrier, 1, device_id=south_id, device_id_type=MESH)

    dyn[...] = jnp.zeros_like(dyn)
    for f in range(3):
        for p in range(16):
            dyn[:, p, f * LANES : f * LANES + NLEV] = gcm_ref[f, :, p * NLEV : (p + 1) * NLEV]

    start = dyn[...].reshape(COLS, 3 * LANES)
    rounded = start.astype(BF16).astype(F32)
    lane = iota((COLS, LANES), 1)
    temper = jnp.where(lane < CZ, rounded[:, 0:LANES], 0.0)
    vapour = jnp.where(lane < CZ, rounded[:, LANES : 2 * LANES], 0.0)
    assigned = asg_ref[...].astype(F32)
    target = jnp.floor((assigned + 0.5) * (1.0 / SLOTS))
    slot = assigned - target * SLOTS + 1.0
    cost = cost_ref[...].astype(F32)
    sub = iota((LANES, COLS), 0)
    labels = jnp.where(sub == LANE_TARGET, target, 0.0)
    labels = jnp.where(sub == LANE_SLOT, slot, labels)
    labels = jnp.where(sub == LANE_COST, cost, labels).astype(BF16)
    eye = one_hot(iota((COLS, COLS), 0) == iota((COLS, COLS), 1))
    payload = temper + pltpu.roll(vapour, 64, 1) + dot_nt(eye, labels)
    got1[me] = payload.astype(BF16)

    wide_lane = iota((COLS, 3 * LANES), 1)
    keep = (wide_lane % LANES) >= CZ
    cloud = wide_lane >= 2 * LANES
    base[...] = jnp.where(keep, -0.5 * rounded, jnp.where(cloud, -rounded, 0.0))

    pl.semaphore_wait(barrier, n_near - 1 + nz - 1 + 2)

    def copy1(o):
        return pltpu.make_async_remote_copy(
            src_ref=got1.at[me],
            dst_ref=got1.at[me],
            send_sem=s1.at[o],
            recv_sem=r1.at[o],
            device_id=near_device((me + o) % n_near),
            device_id_type=MESH,
        )

    for o in range(1, n_near):
        copy1(o).start()

    def edge_copies(turn):
        return [
            pltpu.make_async_remote_copy(
                src_ref=edge_out.at[turn, side],
                dst_ref=edge_in.at[turn, side],
                send_sem=se.at[turn, side],
                recv_sem=re.at[turn, side],
                device_id=(south_id, north_id)[side],
                device_id_type=MESH,
            )
            for side in range(2)
        ]

    weights = edge_weights(nb_ref)

    def dynamics_send(turn):
        for e in range(2):
            local = dot_full(op_ref[e], dyn[e])
            near[16 * e : 16 * e + 16] = local
            edge_out[turn, 0, 4 * e : 4 * e + 4] = local[0:4]
            edge_out[turn, 1, 4 * e : 4 * e + 4] = local[12:16]
        for copy in edge_copies(turn):
            copy.start()

    def dynamics_finish(turn):
        for side, copy in enumerate(edge_copies(turn)):
            copy.wait_recv()
            near[32 + 8 * side : 40 + 8 * side] = edge_in[turn, side]
        dyn[...] = dyn[...] + dot_full(weights, near[...]).reshape(dyn.shape)

    dynamics_send(0)

    wide_row, wide_col = iota((256, 256), 0), iota((256, 256), 1)
    odd = wide_col & 1
    within = (wide_col & 127) >> 1
    regroup = []
    for first in (0, 1):
        side = odd ^ first
        moved = wide_row == 192 * side + within
        meaned = ((wide_row < 64) & (side == 0)) | ((wide_row >= 192) & (side == 1))
        regroup.append(jnp.where(wide_col < 128, jnp.where(moved, 1.0, 0.0), jnp.where(meaned, 1.0 / CX, 0.0)).astype(BF16))
    for f in range(2):
        for g in range(5):
            half_in[40 * f + 8 * g : 40 * f + 8 * g + 8, :] = crm_ref[8 * g : 8 * g + 8, f, :]

    def tile(t):
        return slice(t * LANES, (t + 1) * LANES)

    for j in range(HALF):
        pair = (j // 2, (j + HALF) // 2)
        left, right = pair if j % 2 == 0 else pair[::-1]
        both = jnp.concatenate([half_in[:, tile(left)], half_in[:, tile(right)]], axis=1)
        out = dot(both, regroup[j % 2])
        state_a[0:80, tile(j + 1)] = out[:, 0:LANES]
        drive[:, tile(j)] = out[:, LANES:]
    srow = iota((LANES, LANES), 0) & 63
    scol = iota((LANES, LANES), 1) & 1
    for j in range(HALF):
        spread[:, tile(j)] = one_hot(srow == j + HALF * scol)
    first_means = dot_nt(state_a[0:80, LANES : LANES + WIDE].astype(BF16), spread[...])

    for o in range(1, n_near):
        copy1(o).wait_recv()
    plane = got1[...].reshape(rows1, LANES)
    pick_row = iota((8, LANES), 0)
    pick_lane = iota((8, LANES), 1)
    picker = one_hot(pick_lane == LANE_TARGET + pick_row)
    owner = dot_nt(picker, plane)[0:1, :]
    zid = iota((nz, rows1), 0)
    mine = owner == (x * (2 * nz) + 2 * zid + core).astype(F32)
    hits = jnp.where(mine, 1.0, 0.0)
    before = one_hot(iota((rows1, rows1), 0) < iota((rows1, rows1), 1))
    earlier = dot(hits.astype(BF16), before)
    place = jnp.sum(hits * (zid.astype(F32) * cap2 + earlier + 1.0), axis=0, keepdims=True) - 1.0
    packer = jnp.where(iota((rows2, rows1), 0).astype(F32) == place, 1.0, 0.0)
    pack2[...] = dot(packer.astype(BF16), plane).astype(BF16).reshape(pack2.shape)

    def copy_far(o, src, dst, send, recv):
        to = (z + o) % nz
        return pltpu.make_async_remote_copy(
            src_ref=src.at[to],
            dst_ref=dst.at[z],
            send_sem=send.at[o],
            recv_sem=recv.at[o],
            device_id=far_device(to),
            device_id_type=MESH,
        )

    order = sorted(range(1, nz), key=lambda o: -min(o, nz - o))
    for o in order:
        copy_far(o, pack2, got2, s2, r2).start()
    got2[z] = pack2[z]
    unpacker = packer.T.astype(BF16)

    dynamics_finish(0)
    dynamics_send(1)

    for o in order:
        copy_far(o, pack2, got2, s2, r2).wait_recv()
    arrived = got2[...].reshape(rows2, LANES)
    slot_row = dot_nt(picker, arrived)[1:2, :]
    matcher = one_hot((iota((SLOTS, rows2), 0) + 1).astype(F32) == slot_row)
    forcing = dot(matcher, arrived)
    slot_col = arrived[:, LANE_SLOT : LANE_SLOT + 1].astype(F32)
    matcher_t = one_hot((iota((rows2, LANES), 1) + 1).astype(F32) == slot_col)
    slot_lane = iota((SLOTS, LANES), 1)
    stacked = jnp.concatenate(
        [jnp.where(slot_lane < 64, forcing, 0.0), jnp.where(slot_lane < 64, 0.0, forcing)], axis=0
    ).astype(BF16)
    drive[...] = 0.3 * (dot(stacked, spread[...]) - drive[...])
    near_counts = jnp.broadcast_to(forcing[:, LANE_COST : LANE_COST + 1], (SLOTS, LANES))
    tend[...] = jnp.zeros_like(tend)
    tend[0:SLOTS, 0:LANES] = near_counts

    def slot_group(g, carry):
        top = pl.ds(pl.multiple_of(8 * g, 8), 8)
        low = pl.ds(pl.multiple_of(8 * g + 40, 8), 8)
        last = pl.ds(pl.multiple_of(8 * g + 80, 8), 8)
        steps = tend[top, 0:LANES]
        is_odd = (iota((8, LANES), 1) & 1) == 1
        slope = jnp.where(is_odd, 0.4, 0.0)
        source, sink = state_a, state_b
        for n in range(NSUB):
            active = steps > n + 0.5
            for rows in (top, low):
                first, final = source[rows, tile(1)], source[rows, tile(HALF)]
                source[rows, tile(0)] = jnp.where(is_odd, pltpu.roll(final, 1, 1), first)
                source[rows, tile(HALF + 1)] = jnp.where(is_odd, final, pltpu.roll(first, LANES - 1, 1))
            for j in range(HALF):
                now, mixed = [], []
                for rows in (top, low):
                    own = source[rows, tile(j + 1)]
                    around = (
                        own
                        + source[rows, tile(j)]
                        + source[rows, tile(j + 2)]
                        + pltpu.roll(own, 2, 1)
                        + pltpu.roll(own, LANES - 2, 1)
                    )
                    now.append(own)
                    mixed.append(0.2 * around + drive[rows, tile(j)])
                sat = ((0.5 - 0.8 * j / CZ) - slope) + 0.2 * mixed[0]
                moved = 0.5 * jnp.maximum(mixed[1] - sat, 0.0)
                t_new = jnp.where(active, mixed[0] + moved, now[0])
                w_new = jnp.where(active, mixed[1] - moved, now[1])
                sink[top, tile(j + 1)] = t_new
                sink[low, tile(j + 1)] = w_new
                if n == NSUB - 1:
                    sat = ((0.5 - 0.8 * j / CZ) - slope) + 0.2 * t_new
                    sink[last, tile(j + 1)] = jnp.maximum(w_new - sat, 0.0)
            source, sink = sink, source
        return carry

    lax.fori_loop(0, SLOTS // 8, slot_group, 0)

    final = state_a[:, LANES : LANES + WIDE].astype(BF16)
    means = dot_nt(final, spread[...])
    change = (means[0:80] - first_means) * (1.0 / CX)
    tend[0:SLOTS, 0:LANES] = jnp.where(slot_lane < 64, change[0:40], change[40:80])
    tend[0:SLOTS, LANES:] = means[80:120] * (1.0 / CX)
    pack3[...] = dot(matcher_t, tend[...].astype(BF16)).astype(BF16).reshape(pack3.shape)
    for o in order:
        copy_far(o, pack3, got3, s3, r3).start()
    got3[z] = pack3[z]

    dynamics_finish(1)
    dynamics_send(2)

    back_row, back_col = iota((256, LANES), 0), iota((256, LANES), 1)
    put = 2 * (back_col & 63) + 128 * (back_col >> 6)
    both_low = one_hot(back_row == put)
    both_high = one_hot(back_row == put + 1)
    split = one_hot(back_row == put + (back_col >> 6))
    for t in range(HALF):
        if t < HALF // 2:
            pair, matrix = (2 * t, 2 * t + 1), both_low
        elif t == HALF // 2:
            pair, matrix = (2 * t, 0), split
        else:
            pair, matrix = (2 * t - HALF, 2 * t - HALF + 1), both_high
        both = jnp.concatenate([state_a[0:80, tile(k + 1)] for k in pair], axis=1).astype(BF16)
        half_in[:, tile(t)] = dot(both, matrix).astype(BF16)
    for f in range(2):
        for g in range(5):
            cout_ref[8 * g : 8 * g + 8, f, :] = half_in[40 * f + 8 * g : 40 * f + 8 * g + 8, :]

    for o in order:
        copy_far(o, pack3, got3, s3, r3).wait_recv()
    pack4[...] = dot(unpacker, got3[...].reshape(rows2, 256)).astype(BF16).reshape(pack4.shape)

    def copy4(o):
        to = (me + o) % n_near
        return pltpu.make_async_remote_copy(
            src_ref=pack4.at[to],
            dst_ref=got4.at[me],
            send_sem=s4.at[o],
            recv_sem=r4.at[o],
            device_id=near_device(to),
            device_id_type=MESH,
        )

    for o in range(1, n_near):
        copy4(o).start()
    got4[me] = pack4[me]

    dynamics_finish(2)

    for o in range(1, n_near):
        copy4(o).wait_recv()
    col = got4[0].astype(F32)
    for k in range(1, n_near):
        col = col + got4[k].astype(F32)
    temper = jnp.where(lane < CZ, col[:, 0:LANES], 0.0)
    vapour = jnp.where(lane < CZ, pltpu.roll(col[:, 0:LANES], 64, 1), 0.0)
    cloud = jnp.where(lane < CZ, col[:, LANES:], 0.0)
    gained = jnp.concatenate([temper, vapour, cloud], axis=1) + base[...]
    result = dyn[...] + gained.astype(BF16).astype(F32).reshape(dyn.shape)
    for f in range(3):
        for p in range(16):
            gout_ref[f, :, p * NLEV : (p + 1) * NLEV] = result[:, p, f * LANES : f * LANES + NLEV]

    for o in range(1, n_near):
        copy1(o).wait_send()
        copy4(o).wait_send()
    for o in order:
        copy_far(o, pack2, got2, s2, r2).wait_send()
        copy_far(o, pack3, got3, s3, r3).wait_send()
    for turn in range(NDYN):
        for copy in edge_copies(turn):
            copy.wait_send()


def body(dims, gcm_state, element_op, neighbours, crm_state, assignment, column_cost):
    n_grp, nx, nz, cap = dims
    n_near = 2 * nx
    cap2 = cap * n_near
    vmem = pl.BlockSpec(memory_space=pltpu.VMEM)
    dma = pltpu.SemaphoreType.DMA
    gcm = gcm_state.transpose(1, 0, 2)
    gout, cout = pl.pallas_call(
        functools.partial(kernel, dims),
        out_shape=(
            jax.ShapeDtypeStruct(gcm.shape, F32),
            jax.ShapeDtypeStruct(crm_state.shape, BF16),
        ),
        in_specs=[vmem, vmem, pl.BlockSpec(memory_space=pltpu.SMEM), vmem, vmem, vmem],
        out_specs=(vmem, vmem),
        scratch_shapes=[
            pltpu.VMEM((2, 16, 3 * LANES), F32),
            pltpu.VMEM((COLS, 3 * LANES), F32),
            pltpu.VMEM((48, 3 * LANES), F32),
            pltpu.VMEM((NDYN, 2, 8, 3 * LANES), F32),
            pltpu.VMEM((NDYN, 2, 8, 3 * LANES), F32),
            pltpu.VMEM((n_near, COLS, LANES), BF16),
            pltpu.VMEM((nz, cap2, LANES), BF16),
            pltpu.VMEM((nz, cap2, LANES), BF16),
            pltpu.VMEM((nz, cap2, 2 * LANES), BF16),
            pltpu.VMEM((nz, cap2, 2 * LANES), BF16),
            pltpu.VMEM((n_near, COLS, 2 * LANES), BF16),
            pltpu.VMEM((n_near, COLS, 2 * LANES), BF16),
            pltpu.VMEM((120, WIDE + 2 * LANES), F32),
            pltpu.VMEM((120, WIDE + 2 * LANES), F32),
            pltpu.VMEM((80, WIDE), F32),
            pltpu.VMEM((80, WIDE), BF16),
            pltpu.VMEM((LANES, WIDE), BF16),
            pltpu.VMEM((LANES, 2 * LANES), F32),
            dma((n_near,)),
            dma((n_near,)),
            dma((nz,)),
            dma((nz,)),
            dma((nz,)),
            dma((nz,)),
            dma((n_near,)),
            dma((n_near,)),
            dma((NDYN, 2)),
            dma((NDYN, 2)),
        ],
        compiler_params=pltpu.CompilerParams(
            collective_id=0, has_side_effects=True, vmem_limit_bytes=40 * 2**20
        ),
        name="physics_and_dynamics",
    )(gcm, element_op, neighbours, crm_state, assignment.reshape(1, -1), column_cost.reshape(1, -1))
    return gout.transpose(1, 0, 2), cout


def solution(mesh):
    n_grp, n_dev = mesh.shape["grp"], mesh.shape["dev"]
    nz = 16 if n_dev % 32 == 0 else n_dev // 4
    nx = n_dev // (2 * nz)
    cap = 2 * ((COLS + n_dev - 1) // n_dev)
    in_specs = (
        P(("grp", "dev"), None, None),
        P(("grp", "dev"), None, None),
        P(("grp", "dev"), None),
        P(("grp", "dev"), None, None),
        P(("grp", "dev")),
        P(("grp", "dev")),
    )
    out_specs = (P(("grp", "dev"), None, None), P(("grp", "dev"), None, None))
    return jax.shard_map(
        functools.partial(body, (n_grp, nx, nz, cap)),
        mesh=mesh,
        in_specs=in_specs,
        out_specs=out_specs,
        check_vma=False,
    )
```

```python
import functools

import jax
import jax.numpy as jnp
from jax import lax
from jax.experimental import pallas as pl
from jax.experimental.pallas import tpu as pltpu
from jax.sharding import PartitionSpec as P

NLEV = 72
CZ = 58
CX = 64
HALF = CZ // 2
NSUB = 4
NDYN = 3
COLS = 32
SLOTS = 40
LANES = 128
WIDE = HALF * LANES

MESH = pl.DeviceIdType.MESH
BF16 = jnp.bfloat16
F32 = jnp.float32

LANE_TARGET = 58
LANE_SLOT = 59
LANE_COST = 60


def iota(shape, axis):
    return lax.broadcasted_iota(jnp.int32, shape, axis)


def one_hot(mask, scale=1.0):
    return jnp.where(mask, scale, 0.0).astype(BF16)


def dot(a, b):
    return jnp.dot(a, b, preferred_element_type=F32)


def dot_nt(a, b):
    return lax.dot_general(a, b, (((1,), (1,)), ((), ())), preferred_element_type=F32)


def dot_full(a, b):
    return jnp.dot(a, b, precision=lax.Precision.HIGHEST, preferred_element_type=F32)


def edge_weights(nb_ref):
    shape = (COLS, 48)
    row, col = iota(shape, 0), iota(shape, 1)
    e, p = row // 16, row % 16
    j, i = p // 4, p % 4

    def pick(direction, which):
        first, second = nb_ref[0:1, direction : direction + 1] & 1, nb_ref[1:2, direction : direction + 1] & 1
        return jnp.where(which == 0, first, second)

    east, north, west, south = (pick(d, e) for d in range(4))
    side = jnp.where(i == 3, east, west)
    across = 3 - i
    inner = (i == 1) | (i == 2)
    upper, lower = j == 3, j == 0
    count = jnp.where(col == row, 1.0, 0.0)
    add = lambda total, mask: total + jnp.where(mask, 1.0, 0.0)
    count = add(count, ~inner & (col == side * 16 + j * 4 + across))
    count = add(count, upper & (col == 32 + north * 4 + i))
    count = add(count, lower & (col == 40 + south * 4 + i))
    count = add(count, upper & ~inner & (col == 32 + pick(1, side) * 4 + across))
    count = add(count, lower & ~inner & (col == 40 + pick(3, side) * 4 + across))
    share = jnp.where(inner, 1.0, 0.5) * jnp.where(upper | lower, 0.5, 1.0)
    return count * share * 0.5


def kernel(
    dims,
    gcm_hbm,
    op_hbm,
    nb_hbm,
    crm_hbm,
    asg_hbm,
    cost_hbm,
    gout_ref,
    cout_ref,
    gcm_ref,
    op_ref,
    nb_ref,
    crm_ref,
    asg_ref,
    cost_ref,
    dyn,
    base,
    near,
    edge_out,
    edge_in,
    got1,
    pack2,
    got2,
    pack3,
    got3,
    pack4,
    got4,
    state_a,
    state_b,
    drive,
    half_in,
    spread,
    tend,
    s1,
    r1,
    s2,
    r2,
    s3,
    r3,
    s4,
    r4,
    se,
    re,
    si,
):
    n_grp, nx, nz, cap = dims
    n_near = nx * 2
    n_dev = n_near * nz
    rows1 = n_near * COLS
    cap2 = cap * n_near
    rows2 = nz * cap2
    grp, dev = lax.axis_index("grp"), lax.axis_index("dev")
    core = dev % 2
    z = (dev // 2) % nz
    x = dev // (2 * nz)
    me = x * 2 + core
    flat = grp * n_dev + dev
    total = n_grp * n_dev

    def flat_device(index):
        return (index // n_dev, index % n_dev)

    north_id = flat_device((flat + 1) % total)
    south_id = flat_device((flat + total - 1) % total)

    def near_device(k):
        return (grp, ((k // 2) * nz + z) * 2 + k % 2)

    def far_device(k):
        return (grp, (x * nz + k) * 2 + core)

    barrier = pltpu.get_barrier_semaphore()
    for o in range(1, n_near):
        pl.semaphore_signal(barrier, 1, device_id=near_device((me + o) % n_near), device_id_type=MESH)
    for o in range(1, nz):
        pl.semaphore_signal(barrier, 1, device_id=far_device((z + o) % nz), device_id_type=MESH)
    pl.semaphore_signal(barrier, 1, device_id=north_id, device_id_type=MESH)
    pl.semaphore_signal(barrier, 1, device_id=south_id, device_id_type=MESH)

    loads = {}
    pairs = (
        ("gcm", gcm_hbm, gcm_ref),
        ("asg", asg_hbm, asg_ref),
        ("cost", cost_hbm, cost_ref),
        ("op", op_hbm, op_ref),
        ("nb", nb_hbm, nb_ref),
        ("crm", crm_hbm, crm_ref),
    )
    for number, (which, src, dst) in enumerate(pairs):
        loads[which] = pltpu.make_async_copy(src, dst, si.at[number])
        loads[which].start()

    dyn[...] = jnp.zeros_like(dyn)
    loads["gcm"].wait()
    for f in range(3):
        for p in range(16):
            dyn[:, p, f * LANES : f * LANES + NLEV] = gcm_ref[f, :, p * NLEV : (p + 1) * NLEV]

    start = dyn[...].reshape(COLS, 3 * LANES)
    rounded = start.astype(BF16).astype(F32)
    lane = iota((COLS, LANES), 1)
    temper = jnp.where(lane < CZ, rounded[:, 0:LANES], 0.0)
    vapour = jnp.where(lane < CZ, rounded[:, LANES : 2 * LANES], 0.0)
    loads["asg"].wait()
    loads["cost"].wait()
    assigned = asg_ref[...].astype(F32)
    target = jnp.floor((assigned + 0.5) * (1.0 / SLOTS))
    slot = assigned - target * SLOTS + 1.0
    cost = cost_ref[...].astype(F32)
    sub = iota((LANES, COLS), 0)
    labels = jnp.where(sub == LANE_TARGET, target, 0.0)
    labels = jnp.where(sub == LANE_SLOT, slot, labels)
    labels = jnp.where(sub == LANE_COST, cost, labels).astype(BF16)
    eye = one_hot(iota((COLS, COLS), 0) == iota((COLS, COLS), 1))
    payload = temper + pltpu.roll(vapour, 64, 1) + dot_nt(eye, labels)
    got1[me] = payload.astype(BF16)

    wide_lane = iota((COLS, 3 * LANES), 1)
    keep = (wide_lane % LANES) >= CZ
    cloud = wide_lane >= 2 * LANES
    base[...] = jnp.where(keep, -0.5 * rounded, jnp.where(cloud, -rounded, 0.0))

    pl.semaphore_wait(barrier, n_near - 1 + nz - 1 + 2)

    def copy1(o):
        return pltpu.make_async_remote_copy(
            src_ref=got1.at[me],
            dst_ref=got1.at[me],
            send_sem=s1.at[o],
            recv_sem=r1.at[o],
            device_id=near_device((me + o) % n_near),
            device_id_type=MESH,
        )

    for o in range(1, n_near):
        copy1(o).start()

    def edge_copies(turn):
        return [
            pltpu.make_async_remote_copy(
                src_ref=edge_out.at[turn, side],
                dst_ref=edge_in.at[turn, side],
                send_sem=se.at[turn, side],
                recv_sem=re.at[turn, side],
                device_id=(south_id, north_id)[side],
                device_id_type=MESH,
            )
            for side in range(2)
        ]

    loads["nb"].wait()
    loads["op"].wait()
    weights = edge_weights(nb_ref)

    def dynamics_send(turn):
        for e in range(2):
            local = dot_full(op_ref[e], dyn[e])
            near[16 * e : 16 * e + 16] = local
            edge_out[turn, 0, 4 * e : 4 * e + 4] = local[0:4]
            edge_out[turn, 1, 4 * e : 4 * e + 4] = local[12:16]
        for copy in edge_copies(turn):
            copy.start()

    def dynamics_finish(turn):
        for side, copy in enumerate(edge_copies(turn)):
            copy.wait_recv()
            near[32 + 8 * side : 40 + 8 * side] = edge_in[turn, side]
        dyn[...] = dyn[...] + dot_full(weights, near[...]).reshape(dyn.shape)

    dynamics_send(0)

    wide_row, wide_col = iota((256, 256), 0), iota((256, 256), 1)
    odd = wide_col & 1
    within = (wide_col & 127) >> 1
    regroup = []
    for first in (0, 1):
        side = odd ^ first
        moved = wide_row == 192 * side + within
        meaned = ((wide_row < 64) & (side == 0)) | ((wide_row >= 192) & (side == 1))
        regroup.append(jnp.where(wide_col < 128, jnp.where(moved, 1.0, 0.0), jnp.where(meaned, 1.0 / CX, 0.0)).astype(BF16))
    loads["crm"].wait()
    for f in range(2):
        for g in range(5):
            half_in[40 * f + 8 * g : 40 * f + 8 * g + 8, :] = crm_ref[8 * g : 8 * g + 8, f, :]

    def tile(t):
        return slice(t * LANES, (t + 1) * LANES)

    for j in range(HALF):
        pair = (j // 2, (j + HALF) // 2)
        left, right = pair if j % 2 == 0 else pair[::-1]
        both = jnp.concatenate([half_in[:, tile(left)], half_in[:, tile(right)]], axis=1)
        out = dot(both, regroup[j % 2])
        state_a[0:80, tile(j + 1)] = out[:, 0:LANES]
        drive[:, tile(j)] = out[:, LANES:]
    srow = iota((LANES, LANES), 0) & 63
    scol = iota((LANES, LANES), 1) & 1
    for j in range(HALF):
        spread[:, tile(j)] = one_hot(srow == j + HALF * scol)
    first_means = dot_nt(state_a[0:80, LANES : LANES + WIDE].astype(BF16), spread[...])

    for o in range(1, n_near):
        copy1(o).wait_recv()
    plane = got1[...].reshape(rows1, LANES)
    pick_row = iota((8, LANES), 0)
    pick_lane = iota((8, LANES), 1)
    picker = one_hot(pick_lane == LANE_TARGET + pick_row)
    owner = dot_nt(picker, plane)[0:1, :]
    zid = iota((nz, rows1), 0)
    mine = owner == (x * (2 * nz) + 2 * zid + core).astype(F32)
    hits = jnp.where(mine, 1.0, 0.0)
    before = one_hot(iota((rows1, rows1), 0) < iota((rows1, rows1), 1))
    earlier = dot(hits.astype(BF16), before)
    place = jnp.sum(hits * (zid.astype(F32) * cap2 + earlier + 1.0), axis=0, keepdims=True) - 1.0
    packer = jnp.where(iota((rows2, rows1), 0).astype(F32) == place, 1.0, 0.0)
    pack2[...] = dot(packer.astype(BF16), plane).astype(BF16).reshape(pack2.shape)

    def copy_far(o, src, dst, send, recv):
        to = (z + o) % nz
        return pltpu.make_async_remote_copy(
            src_ref=src.at[to],
            dst_ref=dst.at[z],
            send_sem=send.at[o],
            recv_sem=recv.at[o],
            device_id=far_device(to),
            device_id_type=MESH,
        )

    order = sorted(range(1, nz), key=lambda o: -min(o, nz - o))
    for o in order:
        copy_far(o, pack2, got2, s2, r2).start()
    got2[z] = pack2[z]
    unpacker = packer.T.astype(BF16)

    dynamics_finish(0)
    dynamics_send(1)

    for o in order:
        copy_far(o, pack2, got2, s2, r2).wait_recv()
    arrived = got2[...].reshape(rows2, LANES)
    slot_row = dot_nt(picker, arrived)[1:2, :]
    matcher = one_hot((iota((SLOTS, rows2), 0) + 1).astype(F32) == slot_row)
    forcing = dot(matcher, arrived)
    slot_col = arrived[:, LANE_SLOT : LANE_SLOT + 1].astype(F32)
    matcher_t = one_hot((iota((rows2, LANES), 1) + 1).astype(F32) == slot_col)
    slot_lane = iota((SLOTS, LANES), 1)
    stacked = jnp.concatenate(
        [jnp.where(slot_lane < 64, forcing, 0.0), jnp.where(slot_lane < 64, 0.0, forcing)], axis=0
    ).astype(BF16)
    drive[...] = 0.3 * (dot(stacked, spread[...]) - drive[...])
    near_counts = jnp.broadcast_to(forcing[:, LANE_COST : LANE_COST + 1], (SLOTS, LANES))
    tend[...] = jnp.zeros_like(tend)
    tend[0:SLOTS, 0:LANES] = near_counts

    def slot_group(g):
        top, low, last = (slice(8 * g + 40 * k, 8 * g + 40 * k + 8) for k in range(3))
        steps = tend[top, 0:LANES]
        is_odd = (iota((8, LANES), 1) & 1) == 1
        slope = jnp.where(is_odd, 0.4, 0.0)
        source, sink = state_a, state_b
        for n in range(NSUB):
            active = steps > n + 0.5
            for rows in (top, low):
                first, final = source[rows, tile(1)], source[rows, tile(HALF)]
                source[rows, tile(0)] = jnp.where(is_odd, pltpu.roll(final, 1, 1), first)
                source[rows, tile(HALF + 1)] = jnp.where(is_odd, final, pltpu.roll(first, LANES - 1, 1))
            for j in range(HALF):
                now, mixed = [], []
                for rows in (top, low):
                    own = source[rows, tile(j + 1)]
                    around = (
                        own
                        + source[rows, tile(j)]
                        + source[rows, tile(j + 2)]
                        + pltpu.roll(own, 2, 1)
                        + pltpu.roll(own, LANES - 2, 1)
                    )
                    now.append(own)
                    mixed.append(0.2 * around + drive[rows, tile(j)])
                sat = ((0.5 - 0.8 * j / CZ) - slope) + 0.2 * mixed[0]
                moved = 0.5 * jnp.maximum(mixed[1] - sat, 0.0)
                t_new = jnp.where(active, mixed[0] + moved, now[0])
                w_new = jnp.where(active, mixed[1] - moved, now[1])
                sink[top, tile(j + 1)] = t_new
                sink[low, tile(j + 1)] = w_new
                if n == NSUB - 1:
                    sat = ((0.5 - 0.8 * j / CZ) - slope) + 0.2 * t_new
                    sink[last, tile(j + 1)] = jnp.maximum(w_new - sat, 0.0)
            source, sink = sink, source

    for g in range(SLOTS // 8):
        slot_group(g)

    final = state_a[:, LANES : LANES + WIDE].astype(BF16)
    means = dot_nt(final, spread[...])
    change = (means[0:80] - first_means) * (1.0 / CX)
    tend[0:SLOTS, 0:LANES] = jnp.where(slot_lane < 64, change[0:40], change[40:80])
    tend[0:SLOTS, LANES:] = means[80:120] * (1.0 / CX)
    pack3[...] = dot(matcher_t, tend[...].astype(BF16)).astype(BF16).reshape(pack3.shape)
    for o in order:
        copy_far(o, pack3, got3, s3, r3).start()
    got3[z] = pack3[z]

    dynamics_finish(1)
    dynamics_send(2)

    back_row, back_col = iota((256, LANES), 0), iota((256, LANES), 1)
    put = 2 * (back_col & 63) + 128 * (back_col >> 6)
    both_low = one_hot(back_row == put)
    both_high = one_hot(back_row == put + 1)
    split = one_hot(back_row == put + (back_col >> 6))
    for t in range(HALF):
        if t < HALF // 2:
            pair, matrix = (2 * t, 2 * t + 1), both_low
        elif t == HALF // 2:
            pair, matrix = (2 * t, 0), split
        else:
            pair, matrix = (2 * t - HALF, 2 * t - HALF + 1), both_high
        both = jnp.concatenate([state_a[0:80, tile(k + 1)] for k in pair], axis=1).astype(BF16)
        half_in[:, tile(t)] = dot(both, matrix).astype(BF16)
    for f in range(2):
        for g in range(5):
            cout_ref[8 * g : 8 * g + 8, f, :] = half_in[40 * f + 8 * g : 40 * f + 8 * g + 8, :]

    for o in order:
        copy_far(o, pack3, got3, s3, r3).wait_recv()
    pack4[...] = dot(unpacker, got3[...].reshape(rows2, 256)).astype(BF16).reshape(pack4.shape)

    def copy4(o):
        to = (me + o) % n_near
        return pltpu.make_async_remote_copy(
            src_ref=pack4.at[to],
            dst_ref=got4.at[me],
            send_sem=s4.at[o],
            recv_sem=r4.at[o],
            device_id=near_device(to),
            device_id_type=MESH,
        )

    for o in range(1, n_near):
        copy4(o).start()
    got4[me] = pack4[me]

    dynamics_finish(2)

    for o in range(1, n_near):
        copy4(o).wait_recv()
    col = got4[0].astype(F32)
    for k in range(1, n_near):
        col = col + got4[k].astype(F32)
    temper = jnp.where(lane < CZ, col[:, 0:LANES], 0.0)
    vapour = jnp.where(lane < CZ, pltpu.roll(col[:, 0:LANES], 64, 1), 0.0)
    cloud = jnp.where(lane < CZ, col[:, LANES:], 0.0)
    gained = jnp.concatenate([temper, vapour, cloud], axis=1) + base[...]
    result = dyn[...] + gained.astype(BF16).astype(F32).reshape(dyn.shape)
    for f in range(3):
        for p in range(16):
            gout_ref[f, :, p * NLEV : (p + 1) * NLEV] = result[:, p, f * LANES : f * LANES + NLEV]

    for o in range(1, n_near):
        copy1(o).wait_send()
        copy4(o).wait_send()
    for o in order:
        copy_far(o, pack2, got2, s2, r2).wait_send()
        copy_far(o, pack3, got3, s3, r3).wait_send()
    for turn in range(NDYN):
        for copy in edge_copies(turn):
            copy.wait_send()


def body(dims, gcm_state, element_op, neighbours, crm_state, assignment, column_cost):
    n_grp, nx, nz, cap = dims
    n_near = 2 * nx
    cap2 = cap * n_near
    vmem = pl.BlockSpec(memory_space=pltpu.VMEM)
    dma = pltpu.SemaphoreType.DMA
    gcm = gcm_state.transpose(1, 0, 2)
    gout, cout = pl.pallas_call(
        functools.partial(kernel, dims),
        out_shape=(
            jax.ShapeDtypeStruct(gcm.shape, F32),
            jax.ShapeDtypeStruct(crm_state.shape, BF16),
        ),
        in_specs=[pl.BlockSpec(memory_space=pltpu.HBM)] * 6,
        out_specs=(vmem, vmem),
        scratch_shapes=[
            pltpu.VMEM(gcm.shape, F32),
            pltpu.VMEM(element_op.shape, F32),
            pltpu.VMEM(neighbours.shape, jnp.int32),
            pltpu.VMEM(crm_state.shape, BF16),
            pltpu.VMEM((1, COLS), jnp.int32),
            pltpu.VMEM((1, COLS), jnp.int32),
            pltpu.VMEM((2, 16, 3 * LANES), F32),
            pltpu.VMEM((COLS, 3 * LANES), F32),
            pltpu.VMEM((48, 3 * LANES), F32),
            pltpu.VMEM((NDYN, 2, 8, 3 * LANES), F32),
            pltpu.VMEM((NDYN, 2, 8, 3 * LANES), F32),
            pltpu.VMEM((n_near, COLS, LANES), BF16),
            pltpu.VMEM((nz, cap2, LANES), BF16),
            pltpu.VMEM((nz, cap2, LANES), BF16),
            pltpu.VMEM((nz, cap2, 2 * LANES), BF16),
            pltpu.VMEM((nz, cap2, 2 * LANES), BF16),
            pltpu.VMEM((n_near, COLS, 2 * LANES), BF16),
            pltpu.VMEM((n_near, COLS, 2 * LANES), BF16),
            pltpu.VMEM((120, WIDE + 2 * LANES), F32),
            pltpu.VMEM((120, WIDE + 2 * LANES), F32),
            pltpu.VMEM((80, WIDE), F32),
            pltpu.VMEM((80, WIDE), BF16),
            pltpu.VMEM((LANES, WIDE), BF16),
            pltpu.VMEM((LANES, 2 * LANES), F32),
            dma((n_near,)),
            dma((n_near,)),
            dma((nz,)),
            dma((nz,)),
            dma((nz,)),
            dma((nz,)),
            dma((n_near,)),
            dma((n_near,)),
            dma((NDYN, 2)),
            dma((NDYN, 2)),
            dma((6,)),
        ],
        compiler_params=pltpu.CompilerParams(
            collective_id=0, has_side_effects=True, vmem_limit_bytes=65000 * 1024
        ),
        name="physics_and_dynamics",
    )(gcm, element_op, neighbours, crm_state, assignment.reshape(1, -1), column_cost.reshape(1, -1))
    return gout.transpose(1, 0, 2), cout


def solution(mesh):
    n_grp, n_dev = mesh.shape["grp"], mesh.shape["dev"]
    nz = 16 if n_dev % 32 == 0 else n_dev // 4
    nx = n_dev // (2 * nz)
    cap = 2 * ((COLS + n_dev - 1) // n_dev)
    in_specs = (
        P(("grp", "dev"), None, None),
        P(("grp", "dev"), None, None),
        P(("grp", "dev"), None),
        P(("grp", "dev"), None, None),
        P(("grp", "dev")),
        P(("grp", "dev")),
    )
    out_specs = (P(("grp", "dev"), None, None), P(("grp", "dev"), None, None))
    return jax.shard_map(
        functools.partial(body, (n_grp, nx, nz, cap)),
        mesh=mesh,
        in_specs=in_specs,
        out_specs=out_specs,
        check_vma=False,
    )
```

```python
import functools

import jax
import jax.numpy as jnp
from jax import lax
from jax.experimental import pallas as pl
from jax.experimental.pallas import tpu as pltpu
from jax.sharding import PartitionSpec as P

NLEV = 72
CZ = 58
CX = 64
HALF = CZ // 2
NSUB = 4
NDYN = 3
COLS = 32
SLOTS = 40
LANES = 128
WIDE = HALF * LANES

MESH = pl.DeviceIdType.MESH
BF16 = jnp.bfloat16
F32 = jnp.float32

LANE_TARGET = 58
LANE_SLOT = 59
LANE_COST = 60


def iota(shape, axis):
    return lax.broadcasted_iota(jnp.int32, shape, axis)


def one_hot(mask, scale=1.0):
    return jnp.where(mask, scale, 0.0).astype(BF16)


def dot(a, b):
    return jnp.dot(a, b, preferred_element_type=F32)


def dot_nt(a, b):
    return lax.dot_general(a, b, (((1,), (1,)), ((), ())), preferred_element_type=F32)


def dot_full(a, b):
    return jnp.dot(a, b, precision=lax.Precision.HIGHEST, preferred_element_type=F32)


def edge_weights(nb_ref):
    shape = (COLS, 48)
    row, col = iota(shape, 0), iota(shape, 1)
    e, p = row // 16, row % 16
    j, i = p // 4, p % 4

    def pick(direction, which):
        first, second = nb_ref[0:1, direction : direction + 1] & 1, nb_ref[1:2, direction : direction + 1] & 1
        return jnp.where(which == 0, first, second)

    east, north, west, south = (pick(d, e) for d in range(4))
    side = jnp.where(i == 3, east, west)
    across = 3 - i
    inner = (i == 1) | (i == 2)
    upper, lower = j == 3, j == 0
    count = jnp.where(col == row, 1.0, 0.0)
    add = lambda total, mask: total + jnp.where(mask, 1.0, 0.0)
    count = add(count, ~inner & (col == side * 16 + j * 4 + across))
    count = add(count, upper & (col == 32 + north * 4 + i))
    count = add(count, lower & (col == 40 + south * 4 + i))
    count = add(count, upper & ~inner & (col == 32 + pick(1, side) * 4 + across))
    count = add(count, lower & ~inner & (col == 40 + pick(3, side) * 4 + across))
    share = jnp.where(inner, 1.0, 0.5) * jnp.where(upper | lower, 0.5, 1.0)
    return count * share * 0.5


def kernel(
    dims,
    gcm_hbm,
    op_hbm,
    nb_hbm,
    crm_hbm,
    asg_hbm,
    cost_hbm,
    gout_hbm,
    cout_hbm,
    gout_ref,
    cout_ref,
    gcm_ref,
    op_ref,
    nb_ref,
    crm_ref,
    asg_ref,
    cost_ref,
    dyn,
    base,
    near,
    edge_out,
    edge_in,
    got1,
    pack2,
    got2,
    pack3,
    got3,
    pack4,
    got4,
    state_a,
    state_b,
    drive,
    half_in,
    spread,
    tend,
    s1,
    r1,
    s2,
    r2,
    s3,
    r3,
    s4,
    r4,
    se,
    re,
    si,
    plane_in,
    line_in,
):
    n_grp, nx, nz, cap = dims
    n_near = nx * 2
    n_dev = n_near * nz
    rows1 = n_near * COLS
    cap2 = cap * n_near
    rows2 = nz * cap2
    grp, dev = lax.axis_index("grp"), lax.axis_index("dev")
    core = dev % 2
    z = (dev // 2) % nz
    x = dev // (2 * nz)
    me = x * 2 + core
    flat = grp * n_dev + dev
    total = n_grp * n_dev

    def flat_device(index):
        return (index // n_dev, index % n_dev)

    north_id = flat_device((flat + 1) % total)
    south_id = flat_device((flat + total - 1) % total)

    def near_device(k):
        return (grp, ((k // 2) * nz + z) * 2 + k % 2)

    def far_device(k):
        return (grp, (x * nz + k) * 2 + core)

    def far_line(k):
        return (grp, (x * nz + k % nz) * 2 + 1)

    barrier = pltpu.get_barrier_semaphore()

    def announce(semaphore, device):
        pl.semaphore_signal(semaphore, 1, device_id=device, device_id_type=MESH)

    sibling = near_device(2 * x + 1 - core)
    for o in range(1, nz):
        announce(barrier, far_line(z + o))
    for o in range(1, nx):
        announce(barrier, near_device(2 * ((x + o) % nx)))
    announce(barrier, sibling)
    announce(barrier, north_id)
    announce(barrier, south_id)

    loads = {}
    pairs = (
        ("gcm", gcm_hbm, gcm_ref),
        ("asg", asg_hbm, asg_ref),
        ("cost", cost_hbm, cost_ref),
        ("op", op_hbm, op_ref),
        ("nb", nb_hbm, nb_ref),
        ("crm", crm_hbm, crm_ref),
    )
    for number, (which, src, dst) in enumerate(pairs):
        loads[which] = pltpu.make_async_copy(src, dst, si.at[number])
        loads[which].start()

    dyn[...] = jnp.zeros_like(dyn)
    loads["gcm"].wait()
    for f in range(3):
        for p in range(16):
            dyn[:, p, f * LANES : f * LANES + NLEV] = gcm_ref[f, :, p * NLEV : (p + 1) * NLEV]

    start = dyn[...].reshape(COLS, 3 * LANES)
    rounded = start.astype(BF16).astype(F32)
    lane = iota((COLS, LANES), 1)
    temper = jnp.where(lane < CZ, rounded[:, 0:LANES], 0.0)
    vapour = jnp.where(lane < CZ, rounded[:, LANES : 2 * LANES], 0.0)
    loads["asg"].wait()
    loads["cost"].wait()
    assigned = asg_ref[...].astype(F32)
    target = jnp.floor((assigned + 0.5) * (1.0 / SLOTS))
    slot = assigned - target * SLOTS + 1.0
    cost = cost_ref[...].astype(F32)
    sub = iota((LANES, COLS), 0)
    labels = jnp.where(sub == LANE_TARGET, target, 0.0)
    labels = jnp.where(sub == LANE_SLOT, slot, labels)
    labels = jnp.where(sub == LANE_COST, cost, labels).astype(BF16)
    eye = one_hot(iota((COLS, COLS), 0) == iota((COLS, COLS), 1))
    payload = temper + pltpu.roll(vapour, 64, 1) + dot_nt(eye, labels)
    got1[me] = payload.astype(BF16)

    wide_lane = iota((COLS, 3 * LANES), 1)
    keep = (wide_lane % LANES) >= CZ
    cloud = wide_lane >= 2 * LANES
    base[...] = jnp.where(keep, -0.5 * rounded, jnp.where(cloud, -rounded, 0.0))

    @pl.when(core == 0)
    def _():
        pl.semaphore_wait(barrier, 2 * nx - 1 + 2)
        announce(plane_in, sibling)

    @pl.when(core == 1)
    def _():
        pl.semaphore_wait(plane_in, 1)

    def copy1(o):
        return pltpu.make_async_remote_copy(
            src_ref=got1.at[me],
            dst_ref=got1.at[me],
            send_sem=s1.at[o],
            recv_sem=r1.at[o],
            device_id=near_device((me + o) % n_near),
            device_id_type=MESH,
        )

    for o in range(1, n_near):
        copy1(o).start()

    def edge_copies(turn):
        return [
            pltpu.make_async_remote_copy(
                src_ref=edge_out.at[turn, side],
                dst_ref=edge_in.at[turn, side],
                send_sem=se.at[turn, side],
                recv_sem=re.at[turn, side],
                device_id=(south_id, north_id)[side],
                device_id_type=MESH,
            )
            for side in range(2)
        ]

    loads["nb"].wait()
    loads["op"].wait()
    weights = edge_weights(nb_ref)

    def dynamics_send(turn):
        for e in range(2):
            local = dot_full(op_ref[e], dyn[e])
            near[16 * e : 16 * e + 16] = local
            edge_out[turn, 0, 4 * e : 4 * e + 4] = local[0:4]
            edge_out[turn, 1, 4 * e : 4 * e + 4] = local[12:16]
        for copy in edge_copies(turn):
            copy.start()

    def dynamics_finish(turn):
        for side, copy in enumerate(edge_copies(turn)):
            copy.wait_recv()
            near[32 + 8 * side : 40 + 8 * side] = edge_in[turn, side]
        dyn[...] = dyn[...] + dot_full(weights, near[...]).reshape(dyn.shape)


    wide_row, wide_col = iota((256, 256), 0), iota((256, 256), 1)
    odd = wide_col & 1
    within = (wide_col & 127) >> 1
    regroup = []
    for first in (0, 1):
        side = odd ^ first
        moved = wide_row == 192 * side + within
        meaned = ((wide_row < 64) & (side == 0)) | ((wide_row >= 192) & (side == 1))
        regroup.append(jnp.where(wide_col < 128, jnp.where(moved, 1.0, 0.0), jnp.where(meaned, 1.0 / CX, 0.0)).astype(BF16))
    loads["crm"].wait()
    for f in range(2):
        for g in range(5):
            half_in[40 * f + 8 * g : 40 * f + 8 * g + 8, :] = crm_ref[8 * g : 8 * g + 8, f, :]

    def tile(t):
        return slice(t * LANES, (t + 1) * LANES)

    for j in range(HALF):
        pair = (j // 2, (j + HALF) // 2)
        left, right = pair if j % 2 == 0 else pair[::-1]
        both = jnp.concatenate([half_in[:, tile(left)], half_in[:, tile(right)]], axis=1)
        out = dot(both, regroup[j % 2])
        state_a[0:80, tile(j + 1)] = out[:, 0:LANES]
        drive[:, tile(j)] = out[:, LANES:]
    srow = iota((LANES, LANES), 0) & 63
    scol = iota((LANES, LANES), 1) & 1
    for j in range(HALF):
        spread[:, tile(j)] = one_hot(srow == j + HALF * scol)
    first_means = dot_nt(state_a[0:80, LANES : LANES + WIDE].astype(BF16), spread[...])

    @pl.when(core == 1)
    def _():
        pl.semaphore_wait(barrier, 2 * nz - 1 + 2)
        announce(line_in, sibling)

    dynamics_send(0)

    for o in range(1, n_near):
        copy1(o).wait_recv()
    plane = got1[...].reshape(rows1, LANES)
    pick_row = iota((8, LANES), 0)
    pick_lane = iota((8, LANES), 1)
    picker = one_hot(pick_lane == LANE_TARGET + pick_row)
    owner = dot_nt(picker, plane)[0:1, :]
    zid = iota((nz, rows1), 0)
    mine = owner == (x * (2 * nz) + 2 * zid + core).astype(F32)
    hits = jnp.where(mine, 1.0, 0.0)
    before = one_hot(iota((rows1, rows1), 0) < iota((rows1, rows1), 1))
    earlier = dot(hits.astype(BF16), before)
    place = jnp.sum(hits * (zid.astype(F32) * cap2 + earlier + 1.0), axis=0, keepdims=True) - 1.0
    packer = jnp.where(iota((rows2, rows1), 0).astype(F32) == place, 1.0, 0.0)
    pack2[...] = dot(packer.astype(BF16), plane).astype(BF16).reshape(pack2.shape)

    def copy_far(o, src, dst, send, recv):
        to = (z + o) % nz
        return pltpu.make_async_remote_copy(
            src_ref=src.at[to],
            dst_ref=dst.at[z],
            send_sem=send.at[o],
            recv_sem=recv.at[o],
            device_id=far_device(to),
            device_id_type=MESH,
        )

    order = sorted(range(1, nz), key=lambda o: -min(o, nz - o))
    @pl.when(core == 0)
    def _():
        pl.semaphore_wait(line_in, 1)

    for o in order:
        copy_far(o, pack2, got2, s2, r2).start()
    got2[z] = pack2[z]
    unpacker = packer.T.astype(BF16)

    dynamics_finish(0)
    dynamics_send(1)

    for o in order:
        copy_far(o, pack2, got2, s2, r2).wait_recv()
    arrived = got2[...].reshape(rows2, LANES)
    slot_row = dot_nt(picker, arrived)[1:2, :]
    matcher = one_hot((iota((SLOTS, rows2), 0) + 1).astype(F32) == slot_row)
    forcing = dot(matcher, arrived)
    slot_col = arrived[:, LANE_SLOT : LANE_SLOT + 1].astype(F32)
    matcher_t = one_hot((iota((rows2, LANES), 1) + 1).astype(F32) == slot_col)
    slot_lane = iota((SLOTS, LANES), 1)
    stacked = jnp.concatenate(
        [jnp.where(slot_lane < 64, forcing, 0.0), jnp.where(slot_lane < 64, 0.0, forcing)], axis=0
    ).astype(BF16)
    drive[...] = 0.3 * (dot(stacked, spread[...]) - drive[...])
    near_counts = jnp.broadcast_to(forcing[:, LANE_COST : LANE_COST + 1], (SLOTS, LANES))
    tend[...] = jnp.zeros_like(tend)
    tend[0:SLOTS, 0:LANES] = near_counts

    def slot_group(g):
        top, low, last = (slice(8 * g + 40 * k, 8 * g + 40 * k + 8) for k in range(3))
        steps = tend[top, 0:LANES]
        is_odd = (iota((8, LANES), 1) & 1) == 1
        slope = jnp.where(is_odd, 0.4, 0.0)
        source, sink = state_a, state_b
        for n in range(NSUB):
            active = steps > n + 0.5
            for rows in (top, low):
                first, final = source[rows, tile(1)], source[rows, tile(HALF)]
                source[rows, tile(0)] = jnp.where(is_odd, pltpu.roll(final, 1, 1), first)
                source[rows, tile(HALF + 1)] = jnp.where(is_odd, final, pltpu.roll(first, LANES - 1, 1))
            for j in range(HALF):
                now, mixed = [], []
                for rows in (top, low):
                    own = source[rows, tile(j + 1)]
                    around = (
                        own
                        + source[rows, tile(j)]
                        + source[rows, tile(j + 2)]
                        + pltpu.roll(own, 2, 1)
                        + pltpu.roll(own, LANES - 2, 1)
                    )
                    now.append(own)
                    mixed.append(0.2 * around + drive[rows, tile(j)])
                sat = ((0.5 - 0.8 * j / CZ) - slope) + 0.2 * mixed[0]
                moved = 0.5 * jnp.maximum(mixed[1] - sat, 0.0)
                t_new = jnp.where(active, mixed[0] + moved, now[0])
                w_new = jnp.where(active, mixed[1] - moved, now[1])
                sink[top, tile(j + 1)] = t_new
                sink[low, tile(j + 1)] = w_new
                if n == NSUB - 1:
                    sat = ((0.5 - 0.8 * j / CZ) - slope) + 0.2 * t_new
                    sink[last, tile(j + 1)] = jnp.maximum(w_new - sat, 0.0)
            source, sink = sink, source

    for g in range(SLOTS // 8):
        slot_group(g)

    final = state_a[:, LANES : LANES + WIDE].astype(BF16)
    means = dot_nt(final, spread[...])
    change = (means[0:80] - first_means) * (1.0 / CX)
    tend[0:SLOTS, 0:LANES] = jnp.where(slot_lane < 64, change[0:40], change[40:80])
    tend[0:SLOTS, LANES:] = means[80:120] * (1.0 / CX)
    pack3[...] = dot(matcher_t, tend[...].astype(BF16)).astype(BF16).reshape(pack3.shape)
    for o in order:
        copy_far(o, pack3, got3, s3, r3).start()
    got3[z] = pack3[z]

    dynamics_finish(1)
    dynamics_send(2)

    back_row, back_col = iota((256, LANES), 0), iota((256, LANES), 1)
    put = 2 * (back_col & 63) + 128 * (back_col >> 6)
    both_low = one_hot(back_row == put)
    both_high = one_hot(back_row == put + 1)
    split = one_hot(back_row == put + (back_col >> 6))
    for t in range(HALF):
        if t < HALF // 2:
            pair, matrix = (2 * t, 2 * t + 1), both_low
        elif t == HALF // 2:
            pair, matrix = (2 * t, 0), split
        else:
            pair, matrix = (2 * t - HALF, 2 * t - HALF + 1), both_high
        both = jnp.concatenate([state_a[0:80, tile(k + 1)] for k in pair], axis=1).astype(BF16)
        half_in[:, tile(t)] = dot(both, matrix).astype(BF16)
    for f in range(2):
        for g in range(5):
            cout_ref[8 * g : 8 * g + 8, f, :] = half_in[40 * f + 8 * g : 40 * f + 8 * g + 8, :]
    store_cout = pltpu.make_async_copy(cout_ref, cout_hbm, si.at[6])
    store_cout.start()

    for o in order:
        copy_far(o, pack3, got3, s3, r3).wait_recv()
    pack4[...] = dot(unpacker, got3[...].reshape(rows2, 256)).astype(BF16).reshape(pack4.shape)

    def copy4(o):
        to = (me + o) % n_near
        return pltpu.make_async_remote_copy(
            src_ref=pack4.at[to],
            dst_ref=got4.at[me],
            send_sem=s4.at[o],
            recv_sem=r4.at[o],
            device_id=near_device(to),
            device_id_type=MESH,
        )

    for o in range(1, n_near):
        copy4(o).start()
    got4[me] = pack4[me]

    dynamics_finish(2)

    for o in range(1, n_near):
        copy4(o).wait_recv()
    col = got4[0].astype(F32)
    for k in range(1, n_near):
        col = col + got4[k].astype(F32)
    temper = jnp.where(lane < CZ, col[:, 0:LANES], 0.0)
    vapour = jnp.where(lane < CZ, pltpu.roll(col[:, 0:LANES], 64, 1), 0.0)
    cloud = jnp.where(lane < CZ, col[:, LANES:], 0.0)
    gained = jnp.concatenate([temper, vapour, cloud], axis=1) + base[...]
    result = dyn[...] + gained.astype(BF16).astype(F32).reshape(dyn.shape)
    for f in range(3):
        for p in range(16):
            gout_ref[f, :, p * NLEV : (p + 1) * NLEV] = result[:, p, f * LANES : f * LANES + NLEV]
    store_gout = pltpu.make_async_copy(gout_ref, gout_hbm, si.at[7])
    store_gout.start()

    for o in range(1, n_near):
        copy1(o).wait_send()
        copy4(o).wait_send()
    for o in order:
        copy_far(o, pack2, got2, s2, r2).wait_send()
        copy_far(o, pack3, got3, s3, r3).wait_send()
    for turn in range(NDYN):
        for copy in edge_copies(turn):
            copy.wait_send()
    store_cout.wait()
    store_gout.wait()


PARTS = 2


def hand_over(gout_ref, cout_ref, gout_final, cout_final, gout_mid, cout_mid, sem_in, sem_out):
    chunk = SLOTS // PARTS
    parts = [pl.ds(chunk * g, chunk) for g in range(PARTS)]
    fetch = [pltpu.make_async_copy(cout_ref.at[r], cout_mid.at[r], sem_in.at[g]) for g, r in enumerate(parts)]
    store = [pltpu.make_async_copy(cout_mid.at[r], cout_final.at[r], sem_out.at[g]) for g, r in enumerate(parts)]
    fetch.append(pltpu.make_async_copy(gout_ref, gout_mid, sem_in.at[PARTS]))
    store.append(pltpu.make_async_copy(gout_mid, gout_final, sem_out.at[PARTS]))
    for copy in fetch:
        copy.start()
    for first, second in zip(fetch, store):
        first.wait()
        second.start()
    for copy in store:
        copy.wait()


def body(dims, gcm_state, element_op, neighbours, crm_state, assignment, column_cost):
    n_grp, nx, nz, cap = dims
    n_near = 2 * nx
    cap2 = cap * n_near
    hbm = pl.BlockSpec(memory_space=pltpu.HBM)
    dma = pltpu.SemaphoreType.DMA
    gcm = gcm_state.transpose(1, 0, 2)
    gout, cout = pl.pallas_call(
        functools.partial(kernel, dims),
        out_shape=(
            jax.ShapeDtypeStruct(gcm.shape, F32),
            jax.ShapeDtypeStruct(crm_state.shape, BF16),
        ),
        in_specs=[pl.BlockSpec(memory_space=pltpu.HBM)] * 6,
        out_specs=(hbm, hbm),
        scratch_shapes=[
            pltpu.VMEM(gcm.shape, F32),
            pltpu.VMEM(crm_state.shape, BF16),
            pltpu.VMEM(gcm.shape, F32),
            pltpu.VMEM(element_op.shape, F32),
            pltpu.VMEM(neighbours.shape, jnp.int32),
            pltpu.VMEM(crm_state.shape, BF16),
            pltpu.VMEM((1, COLS), jnp.int32),
            pltpu.VMEM((1, COLS), jnp.int32),
            pltpu.VMEM((2, 16, 3 * LANES), F32),
            pltpu.VMEM((COLS, 3 * LANES), F32),
            pltpu.VMEM((48, 3 * LANES), F32),
            pltpu.VMEM((NDYN, 2, 8, 3 * LANES), F32),
            pltpu.VMEM((NDYN, 2, 8, 3 * LANES), F32),
            pltpu.VMEM((n_near, COLS, LANES), BF16),
            pltpu.VMEM((nz, cap2, LANES), BF16),
            pltpu.VMEM((nz, cap2, LANES), BF16),
            pltpu.VMEM((nz, cap2, 2 * LANES), BF16),
            pltpu.VMEM((nz, cap2, 2 * LANES), BF16),
            pltpu.VMEM((n_near, COLS, 2 * LANES), BF16),
            pltpu.VMEM((n_near, COLS, 2 * LANES), BF16),
            pltpu.VMEM((120, WIDE + 2 * LANES), F32),
            pltpu.VMEM((120, WIDE + 2 * LANES), F32),
            pltpu.VMEM((80, WIDE), F32),
            pltpu.VMEM((80, WIDE), BF16),
            pltpu.VMEM((LANES, WIDE), BF16),
            pltpu.VMEM((LANES, 2 * LANES), F32),
            dma((n_near,)),
            dma((n_near,)),
            dma((nz,)),
            dma((nz,)),
            dma((nz,)),
            dma((nz,)),
            dma((n_near,)),
            dma((n_near,)),
            dma((NDYN, 2)),
            dma((NDYN, 2)),
            dma((8,)),
            pltpu.SemaphoreType.REGULAR,
            pltpu.SemaphoreType.REGULAR,
        ],
        compiler_params=pltpu.CompilerParams(
            collective_id=0, has_side_effects=True, vmem_limit_bytes=65000 * 1024
        ),
        name="physics_and_dynamics",
    )(gcm, element_op, neighbours, crm_state, assignment.reshape(1, -1), column_cost.reshape(1, -1))
    vmem_limit = pltpu.CompilerParams(vmem_limit_bytes=65000 * 1024)
    gout, cout = pl.pallas_call(
        hand_over,
        out_shape=(
            jax.ShapeDtypeStruct(gcm.shape, F32),
            jax.ShapeDtypeStruct(crm_state.shape, BF16),
        ),
        in_specs=[hbm] * 2,
        out_specs=(hbm, hbm),
        scratch_shapes=[
            pltpu.VMEM(gcm.shape, F32),
            pltpu.VMEM(crm_state.shape, BF16),
            dma((1 + PARTS,)),
            dma((1 + PARTS,)),
        ],
        compiler_params=vmem_limit,
        name="hand_over",
    )(gout, cout)
    return gout.transpose(1, 0, 2), cout


def solution(mesh):
    n_grp, n_dev = mesh.shape["grp"], mesh.shape["dev"]
    nz = 16 if n_dev % 32 == 0 else n_dev // 4
    nx = n_dev // (2 * nz)
    cap = 2 * ((COLS + n_dev - 1) // n_dev)
    in_specs = (
        P(("grp", "dev"), None, None),
        P(("grp", "dev"), None, None),
        P(("grp", "dev"), None),
        P(("grp", "dev"), None, None),
        P(("grp", "dev")),
        P(("grp", "dev")),
    )
    out_specs = (P(("grp", "dev"), None, None), P(("grp", "dev"), None, None))
    return jax.shard_map(
        functools.partial(body, (n_grp, nx, nz, cap)),
        mesh=mesh,
        in_specs=in_specs,
        out_specs=out_specs,
        check_vma=False,
    )
```

```python
import functools

import jax
import jax.numpy as jnp
from jax import lax
from jax.experimental import pallas as pl
from jax.experimental.pallas import tpu as pltpu
from jax.sharding import PartitionSpec as P

NLEV = 72
CZ = 58
CX = 64
HALF = CZ // 2
NSUB = 4
NDYN = 3
COLS = 32
SLOTS = 40
LANES = 128
WIDE = HALF * LANES

MESH = pl.DeviceIdType.MESH
BF16 = jnp.bfloat16
F32 = jnp.float32

LANE_PLACE = 58
LANE_CLASS = 59
LANE_SLOT = 60
LANE_COST = 61


def iota(shape, axis):
    return lax.broadcasted_iota(jnp.int32, shape, axis)


def one_hot(mask, scale=1.0):
    return jnp.where(mask, scale, 0.0).astype(BF16)


def dot(a, b):
    return jnp.dot(a, b, preferred_element_type=F32)


def dot_nt(a, b):
    return lax.dot_general(a, b, (((1,), (1,)), ((), ())), preferred_element_type=F32)


def dot_full(a, b):
    return jnp.dot(a, b, precision=lax.Precision.HIGHEST, preferred_element_type=F32)


def edge_weights(nb_ref):
    shape = (COLS, 48)
    row, col = iota(shape, 0), iota(shape, 1)
    e, p = row // 16, row % 16
    j, i = p // 4, p % 4

    def pick(direction, which):
        first, second = nb_ref[0:1, direction : direction + 1] & 1, nb_ref[1:2, direction : direction + 1] & 1
        return jnp.where(which == 0, first, second)

    east, north, west, south = (pick(d, e) for d in range(4))
    side = jnp.where(i == 3, east, west)
    across = 3 - i
    inner = (i == 1) | (i == 2)
    upper, lower = j == 3, j == 0
    count = jnp.where(col == row, 1.0, 0.0)
    add = lambda total, mask: total + jnp.where(mask, 1.0, 0.0)
    count = add(count, ~inner & (col == side * 16 + j * 4 + across))
    count = add(count, upper & (col == 32 + north * 4 + i))
    count = add(count, lower & (col == 40 + south * 4 + i))
    count = add(count, upper & ~inner & (col == 32 + pick(1, side) * 4 + across))
    count = add(count, lower & ~inner & (col == 40 + pick(3, side) * 4 + across))
    share = jnp.where(inner, 1.0, 0.5) * jnp.where(upper | lower, 0.5, 1.0)
    return count * share * 0.5


def kernel(
    dims,
    gcm_hbm,
    op_hbm,
    nb_hbm,
    crm_hbm,
    asg_hbm,
    cost_hbm,
    gout_hbm,
    cout_hbm,
    gout_ref,
    cout_ref,
    gcm_ref,
    op_ref,
    nb_ref,
    crm_ref,
    asg_ref,
    cost_ref,
    dyn,
    base,
    near,
    edge_out,
    edge_in,
    got1,
    pack2,
    got2,
    pack3,
    got3,
    pack4,
    got4,
    state_a,
    state_b,
    drive,
    forced,
    half_in,
    spread,
    tend,
    s1,
    r1,
    s2,
    r2,
    s3,
    r3,
    s4,
    r4,
    se,
    re,
    si,
    plane_in,
    line_in,
):
    n_grp, nx, nz, cap = dims
    n_near = nx * 2
    n_dev = n_near * nz
    rows1 = n_near * COLS
    cap2 = cap * n_near
    rows2 = nz * cap2
    grp, dev = lax.axis_index("grp"), lax.axis_index("dev")
    core = dev % 2
    z = (dev // 2) % nz
    x = dev // (2 * nz)
    me = x * 2 + core
    flat = grp * n_dev + dev
    total = n_grp * n_dev

    def flat_device(index):
        return (index // n_dev, index % n_dev)

    north_id = flat_device((flat + 1) % total)
    south_id = flat_device((flat + total - 1) % total)

    def near_device(k):
        return (grp, ((k // 2) * nz + z) * 2 + k % 2)

    def far_device(k):
        return (grp, (x * nz + k) * 2 + core)

    def far_line(k):
        return (grp, (x * nz + k % nz) * 2 + 1)

    barrier = pltpu.get_barrier_semaphore()

    def announce(semaphore, device):
        pl.semaphore_signal(semaphore, 1, device_id=device, device_id_type=MESH)

    sibling = near_device(2 * x + 1 - core)
    for o in range(1, nz):
        announce(barrier, far_line(z + o))
    for o in range(1, nx):
        announce(barrier, near_device(2 * ((x + o) % nx)))
    announce(barrier, sibling)
    announce(barrier, flat_device((flat + jnp.where(core == 0, total - 1, 2)) % total))

    loads = {}
    pairs = (
        ("gcm", gcm_hbm, gcm_ref),
        ("asg", asg_hbm, asg_ref),
        ("cost", cost_hbm, cost_ref),
        ("op", op_hbm, op_ref),
        ("nb", nb_hbm, nb_ref),
        ("crm", crm_hbm, crm_ref),
    )
    for number, (which, src, dst) in enumerate(pairs):
        loads[which] = pltpu.make_async_copy(src, dst, si.at[number])
        loads[which].start()

    dyn[...] = jnp.zeros_like(dyn)
    loads["gcm"].wait()
    for f in range(3):
        for p in range(16):
            dyn[:, p, f * LANES : f * LANES + NLEV] = gcm_ref[f, :, p * NLEV : (p + 1) * NLEV]

    start = dyn[...].reshape(COLS, 3 * LANES)
    rounded = start.astype(BF16).astype(F32)
    lane = iota((COLS, LANES), 1)
    temper = jnp.where(lane < CZ, rounded[:, 0:LANES], 0.0)
    vapour = jnp.where(lane < CZ, rounded[:, LANES : 2 * LANES], 0.0)
    loads["asg"].wait()
    loads["cost"].wait()
    assigned = asg_ref[...].astype(F32)
    target = jnp.floor((assigned + 0.5) * (1.0 / SLOTS))
    slot = assigned - target * SLOTS + 1.0
    cost = cost_ref[...].astype(F32)
    eye = one_hot(iota((COLS, COLS), 0) == iota((COLS, COLS), 1))
    target_col = dot_nt(eye, jnp.broadcast_to(target, (8, COLS)).astype(BF16))[:, 0:1]
    sooner = iota((COLS, COLS), 0) < iota((COLS, COLS), 1)
    rank = jnp.sum(jnp.where(sooner & (target_col == target), 1.0, 0.0), axis=0, keepdims=True)
    to_x = jnp.floor((target + 0.5) * (1.0 / (2 * nz)))
    rest = target - to_x * (2 * nz)
    to_z = jnp.floor((rest + 0.5) * 0.5)
    kind = to_x * 2.0 + (rest - to_z * 2.0)
    place = to_z * cap2 + (me * cap).astype(F32) + rank
    sub = iota((LANES, COLS), 0)
    labels = jnp.where(sub == LANE_PLACE, place, 0.0)
    labels = jnp.where(sub == LANE_CLASS, kind, labels)
    labels = jnp.where(sub == LANE_SLOT, slot, labels)
    labels = jnp.where(sub == LANE_COST, cost, labels).astype(BF16)
    payload = temper + pltpu.roll(vapour, 64, 1) + dot_nt(eye, labels)
    got1[me] = payload.astype(BF16)

    wide_lane = iota((COLS, 3 * LANES), 1)
    keep = (wide_lane % LANES) >= CZ
    cloud = wide_lane >= 2 * LANES
    base[...] = jnp.where(keep, -0.5 * rounded, jnp.where(cloud, -rounded, 0.0))

    @pl.when(core == 0)
    def _():
        pl.semaphore_wait(barrier, 2 * nx - 1)
        announce(plane_in, sibling)

    @pl.when(core == 1)
    def _():
        pl.semaphore_wait(plane_in, 1)

    def copy1(o):
        return pltpu.make_async_remote_copy(
            src_ref=got1.at[me],
            dst_ref=got1.at[me],
            send_sem=s1.at[o],
            recv_sem=r1.at[o],
            device_id=near_device((me + o) % n_near),
            device_id_type=MESH,
        )

    near_order = sorted(range(1, n_near), key=lambda o: -min(o, n_near - o))
    for o in near_order:
        copy1(o).start()

    def edge_copies(turn):
        return [
            pltpu.make_async_remote_copy(
                src_ref=edge_out.at[turn, side],
                dst_ref=edge_in.at[turn, side],
                send_sem=se.at[turn, side],
                recv_sem=re.at[turn, side],
                device_id=(south_id, north_id)[side],
                device_id_type=MESH,
            )
            for side in range(2)
        ]

    loads["nb"].wait()
    loads["op"].wait()
    weights = edge_weights(nb_ref)

    def dynamics_send(turn):
        for e in range(2):
            local = dot_full(op_ref[e], dyn[e])
            near[16 * e : 16 * e + 16] = local
            edge_out[turn, 0, 4 * e : 4 * e + 4] = local[0:4]
            edge_out[turn, 1, 4 * e : 4 * e + 4] = local[12:16]
        for copy in edge_copies(turn):
            copy.start()

    def dynamics_finish(turn):
        for side, copy in enumerate(edge_copies(turn)):
            copy.wait_recv()
            near[32 + 8 * side : 40 + 8 * side] = edge_in[turn, side]
        dyn[...] = dyn[...] + dot_full(weights, near[...]).reshape(dyn.shape)


    wide_row, wide_col = iota((256, 256), 0), iota((256, 256), 1)
    odd = wide_col & 1
    within = (wide_col & 127) >> 1
    regroup = []
    for first in (0, 1):
        side = odd ^ first
        moved = wide_row == 192 * side + within
        meaned = ((wide_row < 64) & (side == 0)) | ((wide_row >= 192) & (side == 1))
        regroup.append(jnp.where(wide_col < 128, jnp.where(moved, 1.0, 0.0), jnp.where(meaned, 1.0 / CX, 0.0)).astype(BF16))
    loads["crm"].wait()
    for f in range(2):
        for g in range(5):
            half_in[40 * f + 8 * g : 40 * f + 8 * g + 8, :] = crm_ref[8 * g : 8 * g + 8, f, :]

    def tile(t):
        return slice(t * LANES, (t + 1) * LANES)

    for j in range(HALF):
        pair = (j // 2, (j + HALF) // 2)
        left, right = pair if j % 2 == 0 else pair[::-1]
        both = jnp.concatenate([half_in[:, tile(left)], half_in[:, tile(right)]], axis=1)
        out = dot(both, regroup[j % 2])
        state_a[0:80, tile(j + 1)] = out[:, 0:LANES]
        drive[:, tile(j)] = 0.3 * out[:, LANES:]
    srow = iota((LANES, LANES), 0) & 63
    scol = iota((LANES, LANES), 1) & 1
    for j in range(HALF):
        spread[:, tile(j)] = one_hot(srow == j + HALF * scol)
    odd_lane = (iota((8, LANES), 1) & 1) == 1

    def ends(source, rows):
        first, final = source[rows, tile(1)], source[rows, tile(HALF)]
        source[rows, tile(0)] = jnp.where(odd_lane, pltpu.roll(final, 1, 1), first)
        source[rows, tile(HALF + 1)] = jnp.where(odd_lane, final, pltpu.roll(first, LANES - 1, 1))

    def mix(source, rows, j):
        own = source[rows, tile(j + 1)]
        beside = pltpu.roll(own, 2, 1) + pltpu.roll(own, LANES - 2, 1)
        return 0.2 * (own + source[rows, tile(j)] + source[rows, tile(j + 2)] + beside)

    for g in range(2 * SLOTS // 8):
        rows = slice(8 * g, 8 * g + 8)
        ends(state_a, rows)
        for j in range(HALF):
            state_b[rows, tile(j + 1)] = mix(state_a, rows, j) - drive[rows, tile(j)]
    first_means = dot_nt(state_a[0:80, LANES : LANES + WIDE].astype(BF16), spread[...])

    @pl.when(core == 1)
    def _():
        pl.semaphore_wait(barrier, 2 * nz - 1 + 2)
        announce(line_in, sibling)


    for o in range(1, n_near):
        copy1(o).wait_recv()
    plane = got1[...].reshape(rows1, LANES)
    pick_row = iota((8, LANES), 0)
    pick_lane = iota((8, LANES), 1)
    picker = one_hot(pick_lane == LANE_PLACE + pick_row)
    labels = dot_nt(picker, plane)
    place = jnp.where(labels[1:2, :] == me.astype(F32), labels[0:1, :], -1.0)
    packer = one_hot(iota((rows2, rows1), 0).astype(F32) == place)
    pack2[...] = dot(packer, plane).astype(BF16).reshape(pack2.shape)

    def copy_far(o, src, dst, send, recv):
        to = (z + o) % nz
        return pltpu.make_async_remote_copy(
            src_ref=src.at[to],
            dst_ref=dst.at[z],
            send_sem=send.at[o],
            recv_sem=recv.at[o],
            device_id=far_device(to),
            device_id_type=MESH,
        )

    order = sorted(range(1, nz), key=lambda o: -min(o, nz - o))
    @pl.when(core == 0)
    def _():
        pl.semaphore_wait(line_in, 1)

    for o in order:
        copy_far(o, pack2, got2, s2, r2).start()
    got2[z] = pack2[z]
    dynamics_send(0)
    class_col = plane[:, LANE_CLASS : LANE_CLASS + 1].astype(F32)
    place_col = jnp.where(class_col == me.astype(F32), plane[:, LANE_PLACE : LANE_PLACE + 1].astype(F32), -1.0)
    unpacker = one_hot(iota((rows1, rows2), 1).astype(F32) == place_col)

    dynamics_finish(0)
    dynamics_send(1)

    for o in order:
        copy_far(o, pack2, got2, s2, r2).wait_recv()
    arrived = got2[...].reshape(rows2, LANES)
    slot_row = dot_nt(picker, arrived)[2:3, :]
    matcher = one_hot((iota((SLOTS, rows2), 0) + 1).astype(F32) == slot_row)
    forcing = dot(matcher, arrived)
    slot_col = arrived[:, LANE_SLOT : LANE_SLOT + 1].astype(F32)
    matcher_t = one_hot((iota((rows2, LANES), 1) + 1).astype(F32) == slot_col)
    slot_lane = iota((SLOTS, LANES), 1)
    stacked = jnp.concatenate(
        [jnp.where(slot_lane < 64, forcing, 0.0), jnp.where(slot_lane < 64, 0.0, forcing)], axis=0
    ).astype(BF16)
    forced[...] = 0.3 * dot(stacked, spread[...])
    near_counts = jnp.broadcast_to(forcing[:, LANE_COST : LANE_COST + 1], (SLOTS, LANES))
    tend[...] = jnp.zeros_like(tend)
    tend[0:SLOTS, 0:LANES] = near_counts

    def slot_group(g):
        top, low, last = (slice(8 * g + 40 * k, 8 * g + 40 * k + 8) for k in range(3))
        steps = tend[top, 0:LANES]
        slope = jnp.where(odd_lane, 0.4, 0.0)
        source, sink = state_a, state_b
        for n in range(NSUB):
            active = steps > n + 0.5
            if n > 0:
                for rows in (top, low):
                    ends(source, rows)
            for j in range(HALF):
                mixed = []
                for rows in (top, low):
                    if n == 0:
                        mixed.append(state_b[rows, tile(j + 1)] + forced[rows, tile(j)])
                        drive[rows, tile(j)] = forced[rows, tile(j)] - drive[rows, tile(j)]
                    else:
                        mixed.append(mix(source, rows, j) + drive[rows, tile(j)])
                sat = ((0.5 - 0.8 * j / CZ) - slope) + 0.2 * mixed[0]
                moved = 0.5 * jnp.maximum(mixed[1] - sat, 0.0)
                t_new = jnp.where(active, mixed[0] + moved, source[top, tile(j + 1)])
                w_new = jnp.where(active, mixed[1] - moved, source[low, tile(j + 1)])
                sink[top, tile(j + 1)] = t_new
                sink[low, tile(j + 1)] = w_new
                if n == NSUB - 1:
                    sat = ((0.5 - 0.8 * j / CZ) - slope) + 0.2 * t_new
                    sink[last, tile(j + 1)] = jnp.maximum(w_new - sat, 0.0)
            source, sink = sink, source

    for g in range(SLOTS // 8):
        slot_group(g)

    final = state_a[:, LANES : LANES + WIDE].astype(BF16)
    means = dot_nt(final, spread[...])
    change = (means[0:80] - first_means) * (1.0 / CX)
    tend[0:SLOTS, 0:LANES] = jnp.where(slot_lane < 64, change[0:40], change[40:80])
    tend[0:SLOTS, LANES:] = means[80:120] * (1.0 / CX)
    pack3[...] = dot(matcher_t, tend[...].astype(BF16)).astype(BF16).reshape(pack3.shape)
    for o in order:
        copy_far(o, pack3, got3, s3, r3).start()
    got3[z] = pack3[z]

    dynamics_finish(1)
    dynamics_send(2)

    back_row, back_col = iota((256, LANES), 0), iota((256, LANES), 1)
    put = 2 * (back_col & 63) + 128 * (back_col >> 6)
    both_low = one_hot(back_row == put)
    both_high = one_hot(back_row == put + 1)
    split = one_hot(back_row == put + (back_col >> 6))
    for t in range(HALF):
        if t < HALF // 2:
            pair, matrix = (2 * t, 2 * t + 1), both_low
        elif t == HALF // 2:
            pair, matrix = (2 * t, 0), split
        else:
            pair, matrix = (2 * t - HALF, 2 * t - HALF + 1), both_high
        both = jnp.concatenate([state_a[0:80, tile(k + 1)] for k in pair], axis=1).astype(BF16)
        half_in[:, tile(t)] = dot(both, matrix).astype(BF16)
    for f in range(2):
        for g in range(5):
            cout_ref[8 * g : 8 * g + 8, f, :] = half_in[40 * f + 8 * g : 40 * f + 8 * g + 8, :]
    store_cout = pltpu.make_async_copy(cout_ref, cout_hbm, si.at[6])
    store_cout.start()

    for o in order:
        copy_far(o, pack3, got3, s3, r3).wait_recv()
    pack4[...] = dot(unpacker, got3[...].reshape(rows2, 256)).astype(BF16).reshape(pack4.shape)

    def copy4(o):
        to = (me + o) % n_near
        return pltpu.make_async_remote_copy(
            src_ref=pack4.at[to],
            dst_ref=got4.at[me],
            send_sem=s4.at[o],
            recv_sem=r4.at[o],
            device_id=near_device(to),
            device_id_type=MESH,
        )

    for o in near_order:
        copy4(o).start()
    got4[me] = pack4[me]

    dynamics_finish(2)

    for o in range(1, n_near):
        copy4(o).wait_recv()
    col = got4[0].astype(F32)
    for k in range(1, n_near):
        col = col + got4[k].astype(F32)
    temper = jnp.where(lane < CZ, col[:, 0:LANES], 0.0)
    vapour = jnp.where(lane < CZ, pltpu.roll(col[:, 0:LANES], 64, 1), 0.0)
    cloud = jnp.where(lane < CZ, col[:, LANES:], 0.0)
    gained = jnp.concatenate([temper, vapour, cloud], axis=1) + base[...]
    result = dyn[...] + gained.astype(BF16).astype(F32).reshape(dyn.shape)
    for f in range(3):
        for p in range(16):
            gout_ref[f, :, p * NLEV : (p + 1) * NLEV] = result[:, p, f * LANES : f * LANES + NLEV]
    store_gout = pltpu.make_async_copy(gout_ref, gout_hbm, si.at[7])
    store_gout.start()

    for o in range(1, n_near):
        copy1(o).wait_send()
        copy4(o).wait_send()
    for o in order:
        copy_far(o, pack2, got2, s2, r2).wait_send()
        copy_far(o, pack3, got3, s3, r3).wait_send()
    for turn in range(NDYN):
        for copy in edge_copies(turn):
            copy.wait_send()
    store_cout.wait()
    store_gout.wait()


PARTS = 2


def hand_over(gout_ref, cout_ref, gout_final, cout_final, gout_mid, cout_mid, sem_in, sem_out):
    chunk = SLOTS // PARTS
    parts = [pl.ds(chunk * g, chunk) for g in range(PARTS)]
    fetch = [pltpu.make_async_copy(cout_ref.at[r], cout_mid.at[r], sem_in.at[g]) for g, r in enumerate(parts)]
    store = [pltpu.make_async_copy(cout_mid.at[r], cout_final.at[r], sem_out.at[g]) for g, r in enumerate(parts)]
    fetch.append(pltpu.make_async_copy(gout_ref, gout_mid, sem_in.at[PARTS]))
    store.append(pltpu.make_async_copy(gout_mid, gout_final, sem_out.at[PARTS]))
    for copy in fetch:
        copy.start()
    for first, second in zip(fetch, store):
        first.wait()
        second.start()
    for copy in store:
        copy.wait()


def body(dims, gcm_state, element_op, neighbours, crm_state, assignment, column_cost):
    n_grp, nx, nz, cap = dims
    n_near = 2 * nx
    cap2 = cap * n_near
    hbm = pl.BlockSpec(memory_space=pltpu.HBM)
    dma = pltpu.SemaphoreType.DMA
    gcm = gcm_state.transpose(1, 0, 2)
    gout, cout = pl.pallas_call(
        functools.partial(kernel, dims),
        out_shape=(
            jax.ShapeDtypeStruct(gcm.shape, F32),
            jax.ShapeDtypeStruct(crm_state.shape, BF16),
        ),
        in_specs=[pl.BlockSpec(memory_space=pltpu.HBM)] * 6,
        out_specs=(hbm, hbm),
        scratch_shapes=[
            pltpu.VMEM(gcm.shape, F32),
            pltpu.VMEM(crm_state.shape, BF16),
            pltpu.VMEM(gcm.shape, F32),
            pltpu.VMEM(element_op.shape, F32),
            pltpu.VMEM(neighbours.shape, jnp.int32),
            pltpu.VMEM(crm_state.shape, BF16),
            pltpu.VMEM((1, COLS), jnp.int32),
            pltpu.VMEM((1, COLS), jnp.int32),
            pltpu.VMEM((2, 16, 3 * LANES), F32),
            pltpu.VMEM((COLS, 3 * LANES), F32),
            pltpu.VMEM((48, 3 * LANES), F32),
            pltpu.VMEM((NDYN, 2, 8, 3 * LANES), F32),
            pltpu.VMEM((NDYN, 2, 8, 3 * LANES), F32),
            pltpu.VMEM((n_near, COLS, LANES), BF16),
            pltpu.VMEM((nz, cap2, LANES), BF16),
            pltpu.VMEM((nz, cap2, LANES), BF16),
            pltpu.VMEM((nz, cap2, 2 * LANES), BF16),
            pltpu.VMEM((nz, cap2, 2 * LANES), BF16),
            pltpu.VMEM((n_near, COLS, 2 * LANES), BF16),
            pltpu.VMEM((n_near, COLS, 2 * LANES), BF16),
            pltpu.VMEM((120, WIDE + 2 * LANES), F32),
            pltpu.VMEM((120, WIDE + 2 * LANES), F32),
            pltpu.VMEM((80, WIDE), F32),
            pltpu.VMEM((80, WIDE), F32),
            pltpu.VMEM((80, WIDE), BF16),
            pltpu.VMEM((LANES, WIDE), BF16),
            pltpu.VMEM((LANES, 2 * LANES), F32),
            dma((n_near,)),
            dma((n_near,)),
            dma((nz,)),
            dma((nz,)),
            dma((nz,)),
            dma((nz,)),
            dma((n_near,)),
            dma((n_near,)),
            dma((NDYN, 2)),
            dma((NDYN, 2)),
            dma((8,)),
            pltpu.SemaphoreType.REGULAR,
            pltpu.SemaphoreType.REGULAR,
        ],
        compiler_params=pltpu.CompilerParams(
            collective_id=0, has_side_effects=True, vmem_limit_bytes=65000 * 1024
        ),
        name="physics_and_dynamics",
    )(gcm, element_op, neighbours, crm_state, assignment.reshape(1, -1), column_cost.reshape(1, -1))
    vmem_limit = pltpu.CompilerParams(vmem_limit_bytes=65000 * 1024)
    gout, cout = pl.pallas_call(
        hand_over,
        out_shape=(
            jax.ShapeDtypeStruct(gcm.shape, F32),
            jax.ShapeDtypeStruct(crm_state.shape, BF16),
        ),
        in_specs=[hbm] * 2,
        out_specs=(hbm, hbm),
        scratch_shapes=[
            pltpu.VMEM(gcm.shape, F32),
            pltpu.VMEM(crm_state.shape, BF16),
            dma((1 + PARTS,)),
            dma((1 + PARTS,)),
        ],
        compiler_params=vmem_limit,
        name="hand_over",
    )(gout, cout)
    return gout.transpose(1, 0, 2), cout


def solution(mesh):
    n_grp, n_dev = mesh.shape["grp"], mesh.shape["dev"]
    nz = 16 if n_dev % 32 == 0 else n_dev // 4
    nx = n_dev // (2 * nz)
    cap = 2 * ((COLS + n_dev - 1) // n_dev)
    in_specs = (
        P(("grp", "dev"), None, None),
        P(("grp", "dev"), None, None),
        P(("grp", "dev"), None),
        P(("grp", "dev"), None, None),
        P(("grp", "dev")),
        P(("grp", "dev")),
    )
    out_specs = (P(("grp", "dev"), None, None), P(("grp", "dev"), None, None))
    return jax.shard_map(
        functools.partial(body, (n_grp, nx, nz, cap)),
        mesh=mesh,
        in_specs=in_specs,
        out_specs=out_specs,
        check_vma=False,
    )
```

```python
import functools

import jax
import jax.numpy as jnp
from jax import lax
from jax.experimental import pallas as pl
from jax.experimental.pallas import tpu as pltpu
from jax.sharding import PartitionSpec as P

NLEV = 72
CZ = 58
CX = 64
HALF = CZ // 2
NSUB = 4
NDYN = 3
COLS = 32
SLOTS = 40
LANES = 128
WIDE = HALF * LANES

MESH = pl.DeviceIdType.MESH
BF16 = jnp.bfloat16
F32 = jnp.float32

LANE_PLACE = 58
LANE_CLASS = 59
LANE_SLOT = 60
LANE_COST = 61


def iota(shape, axis):
    return lax.broadcasted_iota(jnp.int32, shape, axis)


def one_hot(mask, scale=1.0):
    return jnp.where(mask, scale, 0.0).astype(BF16)


def dot(a, b):
    return jnp.dot(a, b, preferred_element_type=F32)


def dot_nt(a, b):
    return lax.dot_general(a, b, (((1,), (1,)), ((), ())), preferred_element_type=F32)


def dot_full(a, b):
    return jnp.dot(a, b, precision=lax.Precision.HIGHEST, preferred_element_type=F32)


def edge_weights(nb_ref):
    shape = (COLS, 48)
    row, col = iota(shape, 0), iota(shape, 1)
    e, p = row // 16, row % 16
    j, i = p // 4, p % 4

    def pick(direction, which):
        first, second = nb_ref[0:1, direction : direction + 1] & 1, nb_ref[1:2, direction : direction + 1] & 1
        return jnp.where(which == 0, first, second)

    east, north, west, south = (pick(d, e) for d in range(4))
    side = jnp.where(i == 3, east, west)
    across = 3 - i
    inner = (i == 1) | (i == 2)
    upper, lower = j == 3, j == 0
    count = jnp.where(col == row, 1.0, 0.0)
    add = lambda total, mask: total + jnp.where(mask, 1.0, 0.0)
    count = add(count, ~inner & (col == side * 16 + j * 4 + across))
    count = add(count, upper & (col == 32 + north * 4 + i))
    count = add(count, lower & (col == 40 + south * 4 + i))
    count = add(count, upper & ~inner & (col == 32 + pick(1, side) * 4 + across))
    count = add(count, lower & ~inner & (col == 40 + pick(3, side) * 4 + across))
    share = jnp.where(inner, 1.0, 0.5) * jnp.where(upper | lower, 0.5, 1.0)
    return count * share * 0.5


def kernel(
    dims,
    gcm_hbm,
    op_hbm,
    nb_hbm,
    crm_hbm,
    asg_hbm,
    cost_hbm,
    gout_hbm,
    cout_hbm,
    gout_ref,
    cout_ref,
    gcm_ref,
    op_ref,
    nb_ref,
    crm_ref,
    asg_ref,
    cost_ref,
    dyn,
    base,
    near,
    edge_out,
    edge_in,
    got1,
    pack2,
    got2,
    pack3,
    got3,
    pack4,
    got4,
    state_a,
    state_b,
    drive,
    forced,
    half_in,
    spread,
    tend,
    s1,
    r1,
    s2,
    r2,
    s3,
    r3,
    s4,
    r4,
    se,
    re,
    si,
    plane_in,
    line_in,
):
    n_grp, nx, nz, cap = dims
    n_near = nx * 2
    n_dev = n_near * nz
    rows1 = n_near * COLS
    cap2 = cap * n_near
    rows2 = nz * cap2
    grp, dev = lax.axis_index("grp"), lax.axis_index("dev")
    core = dev % 2
    z = (dev // 2) % nz
    x = dev // (2 * nz)
    me = x * 2 + core
    flat = grp * n_dev + dev
    total = n_grp * n_dev

    def flat_device(index):
        return (index // n_dev, index % n_dev)

    north_id = flat_device((flat + 1) % total)
    south_id = flat_device((flat + total - 1) % total)

    def near_device(k):
        return (grp, ((k // 2) * nz + z) * 2 + k % 2)

    def far_device(k):
        return (grp, (x * nz + k) * 2 + core)

    def far_line(k):
        return (grp, (x * nz + k % nz) * 2 + 1)

    barrier = pltpu.get_barrier_semaphore()

    def announce(semaphore, device):
        pl.semaphore_signal(semaphore, 1, device_id=device, device_id_type=MESH)

    sibling = near_device(2 * x + 1 - core)
    for o in range(1, nz):
        announce(barrier, far_line(z + o))
    for o in range(1, nx):
        announce(barrier, near_device(2 * ((x + o) % nx)))
    announce(barrier, sibling)
    announce(barrier, flat_device((flat + jnp.where(core == 0, total - 1, 2)) % total))

    loads = {}
    pairs = (
        ("gcm", gcm_hbm, gcm_ref),
        ("asg", asg_hbm, asg_ref),
        ("cost", cost_hbm, cost_ref),
        ("op", op_hbm, op_ref),
        ("nb", nb_hbm, nb_ref),
        ("crm", crm_hbm, crm_ref),
    )
    for number, (which, src, dst) in enumerate(pairs):
        loads[which] = pltpu.make_async_copy(src, dst, si.at[number])
        loads[which].start()

    dyn[...] = jnp.zeros_like(dyn)
    loads["gcm"].wait()
    for f in range(3):
        for p in range(16):
            dyn[:, p, f * LANES : f * LANES + NLEV] = gcm_ref[f, :, p * NLEV : (p + 1) * NLEV]

    start = dyn[...].reshape(COLS, 3 * LANES)
    rounded = start.astype(BF16).astype(F32)
    lane = iota((COLS, LANES), 1)
    temper = jnp.where(lane < CZ, rounded[:, 0:LANES], 0.0)
    vapour = jnp.where(lane < CZ, rounded[:, LANES : 2 * LANES], 0.0)
    loads["asg"].wait()
    loads["cost"].wait()
    assigned = asg_ref[...].astype(F32)
    target = jnp.floor((assigned + 0.5) * (1.0 / SLOTS))
    slot = assigned - target * SLOTS + 1.0
    cost = cost_ref[...].astype(F32)
    eye = one_hot(iota((COLS, COLS), 0) == iota((COLS, COLS), 1))
    target_col = dot_nt(eye, jnp.broadcast_to(target, (8, COLS)).astype(BF16))[:, 0:1]
    sooner = iota((COLS, COLS), 0) < iota((COLS, COLS), 1)
    rank = jnp.sum(jnp.where(sooner & (target_col == target), 1.0, 0.0), axis=0, keepdims=True)
    to_x = jnp.floor((target + 0.5) * (1.0 / (2 * nz)))
    rest = target - to_x * (2 * nz)
    to_z = jnp.floor((rest + 0.5) * 0.5)
    kind = to_x * 2.0 + (rest - to_z * 2.0)
    place = to_z * cap2 + (me * cap).astype(F32) + rank
    sub = iota((LANES, COLS), 0)
    labels = jnp.where(sub == LANE_PLACE, place, 0.0)
    labels = jnp.where(sub == LANE_CLASS, kind, labels)
    labels = jnp.where(sub == LANE_SLOT, slot, labels)
    labels = jnp.where(sub == LANE_COST, cost, labels).astype(BF16)
    payload = temper + pltpu.roll(vapour, 64, 1) + dot_nt(eye, labels)
    got1[me] = payload.astype(BF16)

    wide_lane = iota((COLS, 3 * LANES), 1)
    keep = (wide_lane % LANES) >= CZ
    cloud = wide_lane >= 2 * LANES
    base[...] = jnp.where(keep, -0.5 * rounded, jnp.where(cloud, -rounded, 0.0))

    @pl.when(core == 0)
    def _():
        pl.semaphore_wait(barrier, 2 * nx - 1)
        announce(plane_in, sibling)

    @pl.when(core == 1)
    def _():
        pl.semaphore_wait(plane_in, 1)

    def copy1(o):
        return pltpu.make_async_remote_copy(
            src_ref=got1.at[me],
            dst_ref=got1.at[me],
            send_sem=s1.at[o],
            recv_sem=r1.at[o],
            device_id=near_device((me + o) % n_near),
            device_id_type=MESH,
        )

    near_order = sorted(range(1, n_near), key=lambda o: -min(o, n_near - o))
    for o in near_order:
        copy1(o).start()

    def edge_copies(turn):
        return [
            pltpu.make_async_remote_copy(
                src_ref=edge_out.at[turn, side],
                dst_ref=edge_in.at[turn, side],
                send_sem=se.at[turn, side],
                recv_sem=re.at[turn, side],
                device_id=(south_id, north_id)[side],
                device_id_type=MESH,
            )
            for side in range(2)
        ]

    loads["nb"].wait()
    loads["op"].wait()
    weights = edge_weights(nb_ref)

    def dynamics_send(turn):
        for e in range(2):
            local = dot_full(op_ref[e], dyn[e])
            near[16 * e : 16 * e + 16] = local
            edge_out[turn, 0, 4 * e : 4 * e + 4] = local[0:4]
            edge_out[turn, 1, 4 * e : 4 * e + 4] = local[12:16]
        for copy in edge_copies(turn):
            copy.start()

    def dynamics_finish(turn):
        for side, copy in enumerate(edge_copies(turn)):
            copy.wait_recv()
            near[32 + 8 * side : 40 + 8 * side] = edge_in[turn, side]
        dyn[...] = dyn[...] + dot_full(weights, near[...]).reshape(dyn.shape)


    wide_row, wide_col = iota((256, 256), 0), iota((256, 256), 1)
    odd = wide_col & 1
    within = (wide_col & 127) >> 1
    regroup = []
    for first in (0, 1):
        side = odd ^ first
        moved = wide_row == 192 * side + within
        meaned = ((wide_row < 64) & (side == 0)) | ((wide_row >= 192) & (side == 1))
        regroup.append(jnp.where(wide_col < 128, jnp.where(moved, 1.0, 0.0), jnp.where(meaned, 1.0 / CX, 0.0)).astype(BF16))
    loads["crm"].wait()
    for f in range(2):
        for g in range(5):
            half_in[40 * f + 8 * g : 40 * f + 8 * g + 8, :] = crm_ref[8 * g : 8 * g + 8, f, :]

    def tile(t):
        return slice(t * LANES, (t + 1) * LANES)

    for j in range(HALF):
        pair = (j // 2, (j + HALF) // 2)
        left, right = pair if j % 2 == 0 else pair[::-1]
        both = jnp.concatenate([half_in[:, tile(left)], half_in[:, tile(right)]], axis=1)
        out = dot(both, regroup[j % 2])
        state_a[0:80, tile(j + 1)] = out[:, 0:LANES]
        drive[:, tile(j)] = 0.3 * out[:, LANES:]
    srow = iota((LANES, LANES), 0) & 63
    scol = iota((LANES, LANES), 1) & 1
    for j in range(HALF):
        spread[:, tile(j)] = one_hot(srow == j + HALF * scol)
    odd_lane = (iota((8, LANES), 1) & 1) == 1

    def ends(source, rows):
        first, final = source[rows, tile(1)], source[rows, tile(HALF)]
        source[rows, tile(0)] = jnp.where(odd_lane, pltpu.roll(final, 1, 1), first)
        source[rows, tile(HALF + 1)] = jnp.where(odd_lane, final, pltpu.roll(first, LANES - 1, 1))

    def mix(source, rows, j):
        own = source[rows, tile(j + 1)]
        beside = pltpu.roll(own, 2, 1) + pltpu.roll(own, LANES - 2, 1)
        return 0.2 * (own + source[rows, tile(j)] + source[rows, tile(j + 2)] + beside)

    for g in range(2 * SLOTS // 8):
        rows = slice(8 * g, 8 * g + 8)
        ends(state_a, rows)
        for j in range(HALF):
            state_b[rows, tile(j + 1)] = mix(state_a, rows, j) - drive[rows, tile(j)]
    first_means = dot_nt(state_a[0:80, LANES : LANES + WIDE].astype(BF16), spread[...])

    @pl.when(core == 1)
    def _():
        pl.semaphore_wait(barrier, 2 * nz - 1 + 2)
        announce(line_in, sibling)


    for o in range(1, n_near):
        copy1(o).wait_recv()
    plane = got1[...].reshape(rows1, LANES)
    pick_row = iota((8, LANES), 0)
    pick_lane = iota((8, LANES), 1)
    picker = one_hot(pick_lane == LANE_PLACE + pick_row)
    labels = dot_nt(picker, plane)
    place = jnp.where(labels[1:2, :] == me.astype(F32), labels[0:1, :], -1.0)
    packer = one_hot(iota((rows2, rows1), 0).astype(F32) == place)
    pack2[...] = dot(packer, plane).astype(BF16).reshape(pack2.shape)

    def copy_far(o, src, dst, send, recv):
        to = (z + o) % nz
        return pltpu.make_async_remote_copy(
            src_ref=src.at[to],
            dst_ref=dst.at[z],
            send_sem=send.at[o],
            recv_sem=recv.at[o],
            device_id=far_device(to),
            device_id_type=MESH,
        )

    order = sorted(range(1, nz), key=lambda o: -min(o, nz - o))
    @pl.when(core == 0)
    def _():
        pl.semaphore_wait(line_in, 1)

    for o in order:
        copy_far(o, pack2, got2, s2, r2).start()
    got2[z] = pack2[z]
    dynamics_send(0)
    class_col = plane[:, LANE_CLASS : LANE_CLASS + 1].astype(F32)
    place_col = jnp.where(class_col == me.astype(F32), plane[:, LANE_PLACE : LANE_PLACE + 1].astype(F32), -1.0)
    unpacker = one_hot(iota((rows1, rows2), 1).astype(F32) == place_col)

    dynamics_finish(0)
    dynamics_send(1)

    for o in order:
        copy_far(o, pack2, got2, s2, r2).wait_recv()
    arrived = got2[...].reshape(rows2, LANES)
    slot_row = dot_nt(picker, arrived)[2:3, :]
    matcher = one_hot((iota((SLOTS, rows2), 0) + 1).astype(F32) == slot_row)
    forcing = dot(matcher, arrived)
    slot_col = arrived[:, LANE_SLOT : LANE_SLOT + 1].astype(F32)
    matcher_t = one_hot((iota((rows2, LANES), 1) + 1).astype(F32) == slot_col)
    slot_lane = iota((SLOTS, LANES), 1)
    stacked = jnp.concatenate(
        [jnp.where(slot_lane < 64, forcing, 0.0), jnp.where(slot_lane < 64, 0.0, forcing)], axis=0
    ).astype(BF16)
    forced[...] = 0.3 * dot(stacked, spread[...])
    near_counts = jnp.broadcast_to(forcing[:, LANE_COST : LANE_COST + 1], (SLOTS, LANES))
    tend[...] = jnp.zeros_like(tend)
    tend[0:SLOTS, 0:LANES] = near_counts

    def slot_group(g):
        top, low, last = (slice(8 * g + 40 * k, 8 * g + 40 * k + 8) for k in range(3))
        steps = tend[top, 0:LANES]
        slope = jnp.where(odd_lane, 0.4, 0.0)
        source, sink = state_a, state_b
        for n in range(NSUB):
            active = steps > n + 0.5
            if n > 0:
                for rows in (top, low):
                    ends(source, rows)
            for j in range(HALF):
                mixed = []
                for rows in (top, low):
                    if n == 0:
                        mixed.append(state_b[rows, tile(j + 1)] + forced[rows, tile(j)])
                        drive[rows, tile(j)] = forced[rows, tile(j)] - drive[rows, tile(j)]
                    else:
                        mixed.append(mix(source, rows, j) + drive[rows, tile(j)])
                sat = ((0.5 - 0.8 * j / CZ) - slope) + 0.2 * mixed[0]
                moved = 0.5 * jnp.maximum(mixed[1] - sat, 0.0)
                t_new = jnp.where(active, mixed[0] + moved, source[top, tile(j + 1)])
                w_new = jnp.where(active, mixed[1] - moved, source[low, tile(j + 1)])
                sink[top, tile(j + 1)] = t_new
                sink[low, tile(j + 1)] = w_new
                if n == NSUB - 1:
                    sat = ((0.5 - 0.8 * j / CZ) - slope) + 0.2 * t_new
                    sink[last, tile(j + 1)] = jnp.maximum(w_new - sat, 0.0)
            source, sink = sink, source

    for g in range(SLOTS // 8):
        slot_group(g)

    final = state_a[:, LANES : LANES + WIDE].astype(BF16)
    means = dot_nt(final, spread[...])
    change = (means[0:80] - first_means) * (1.0 / CX)
    tend[0:SLOTS, 0:LANES] = jnp.where(slot_lane < 64, change[0:40], change[40:80])
    tend[0:SLOTS, LANES:] = means[80:120] * (1.0 / CX)
    pack3[...] = dot(matcher_t, tend[...].astype(BF16)).astype(BF16).reshape(pack3.shape)
    for o in order:
        copy_far(o, pack3, got3, s3, r3).start()
    got3[z] = pack3[z]

    dynamics_finish(1)
    dynamics_send(2)

    back_row, back_col = iota((256, LANES), 0), iota((256, LANES), 1)
    put = 2 * (back_col & 63) + 128 * (back_col >> 6)
    both_low = one_hot(back_row == put)
    both_high = one_hot(back_row == put + 1)
    split = one_hot(back_row == put + (back_col >> 6))
    for t in range(HALF):
        if t < HALF // 2:
            pair, matrix = (2 * t, 2 * t + 1), both_low
        elif t == HALF // 2:
            pair, matrix = (2 * t, 0), split
        else:
            pair, matrix = (2 * t - HALF, 2 * t - HALF + 1), both_high
        both = jnp.concatenate([state_a[0:80, tile(k + 1)] for k in pair], axis=1).astype(BF16)
        half_in[:, tile(t)] = dot(both, matrix).astype(BF16)
    for f in range(2):
        for g in range(5):
            cout_ref[8 * g : 8 * g + 8, f, :] = half_in[40 * f + 8 * g : 40 * f + 8 * g + 8, :]
    store_cout = pltpu.make_async_copy(cout_ref, cout_hbm, si.at[6])
    store_cout.start()

    for o in order:
        copy_far(o, pack3, got3, s3, r3).wait_recv()
    home = dot(unpacker, got3[...].reshape(rows2, 2 * LANES)).reshape(n_near, COLS, 2 * LANES)
    pack4[:, 0:COLS] = home[:, :, 0:LANES].astype(BF16)
    water = home[:, :, LANES:]
    first_half = iota((n_near, 16, LANES), 2) < 64
    pack4[:, COLS:48] = jnp.where(first_half, water[:, 0:16], water[:, 16:32]).astype(BF16)

    def copy4(o):
        to = (me + o) % n_near
        return pltpu.make_async_remote_copy(
            src_ref=pack4.at[to],
            dst_ref=got4.at[me],
            send_sem=s4.at[o],
            recv_sem=r4.at[o],
            device_id=near_device(to),
            device_id_type=MESH,
        )

    for o in near_order:
        copy4(o).start()
    got4[me] = pack4[me]

    dynamics_finish(2)

    for o in range(1, n_near):
        copy4(o).wait_recv()
    col = got4[0].astype(F32)
    for k in range(1, n_near):
        col = col + got4[k].astype(F32)
    temper = jnp.where(lane < CZ, col[0:COLS], 0.0)
    vapour = jnp.where(lane < CZ, pltpu.roll(col[0:COLS], 64, 1), 0.0)
    water = jnp.concatenate([col[COLS:48], pltpu.roll(col[COLS:48], 64, 1)], axis=0)
    cloud = jnp.where(lane < CZ, water, 0.0)
    gained = jnp.concatenate([temper, vapour, cloud], axis=1) + base[...]
    result = dyn[...] + gained.astype(BF16).astype(F32).reshape(dyn.shape)
    for f in range(3):
        for p in range(16):
            gout_ref[f, :, p * NLEV : (p + 1) * NLEV] = result[:, p, f * LANES : f * LANES + NLEV]
    store_gout = pltpu.make_async_copy(gout_ref, gout_hbm, si.at[7])
    store_gout.start()

    for o in range(1, n_near):
        copy1(o).wait_send()
        copy4(o).wait_send()
    for o in order:
        copy_far(o, pack2, got2, s2, r2).wait_send()
        copy_far(o, pack3, got3, s3, r3).wait_send()
    for turn in range(NDYN):
        for copy in edge_copies(turn):
            copy.wait_send()
    store_cout.wait()
    store_gout.wait()


PARTS = 2


def hand_over(gout_ref, cout_ref, gout_final, cout_final, gout_mid, cout_mid, sem_in, sem_out):
    chunk = SLOTS // PARTS
    parts = [pl.ds(chunk * g, chunk) for g in range(PARTS)]
    fetch = [pltpu.make_async_copy(cout_ref.at[r], cout_mid.at[r], sem_in.at[g]) for g, r in enumerate(parts)]
    store = [pltpu.make_async_copy(cout_mid.at[r], cout_final.at[r], sem_out.at[g]) for g, r in enumerate(parts)]
    fetch.append(pltpu.make_async_copy(gout_ref, gout_mid, sem_in.at[PARTS]))
    store.append(pltpu.make_async_copy(gout_mid, gout_final, sem_out.at[PARTS]))
    for copy in fetch:
        copy.start()
    for first, second in zip(fetch, store):
        first.wait()
        second.start()
    for copy in store:
        copy.wait()


def body(dims, gcm_state, element_op, neighbours, crm_state, assignment, column_cost):
    n_grp, nx, nz, cap = dims
    n_near = 2 * nx
    cap2 = cap * n_near
    hbm = pl.BlockSpec(memory_space=pltpu.HBM)
    dma = pltpu.SemaphoreType.DMA
    gcm = gcm_state.transpose(1, 0, 2)
    gout, cout = pl.pallas_call(
        functools.partial(kernel, dims),
        out_shape=(
            jax.ShapeDtypeStruct(gcm.shape, F32),
            jax.ShapeDtypeStruct(crm_state.shape, BF16),
        ),
        in_specs=[pl.BlockSpec(memory_space=pltpu.HBM)] * 6,
        out_specs=(hbm, hbm),
        scratch_shapes=[
            pltpu.VMEM(gcm.shape, F32),
            pltpu.VMEM(crm_state.shape, BF16),
            pltpu.VMEM(gcm.shape, F32),
            pltpu.VMEM(element_op.shape, F32),
            pltpu.VMEM(neighbours.shape, jnp.int32),
            pltpu.VMEM(crm_state.shape, BF16),
            pltpu.VMEM((1, COLS), jnp.int32),
            pltpu.VMEM((1, COLS), jnp.int32),
            pltpu.VMEM((2, 16, 3 * LANES), F32),
            pltpu.VMEM((COLS, 3 * LANES), F32),
            pltpu.VMEM((48, 3 * LANES), F32),
            pltpu.VMEM((NDYN, 2, 8, 3 * LANES), F32),
            pltpu.VMEM((NDYN, 2, 8, 3 * LANES), F32),
            pltpu.VMEM((n_near, COLS, LANES), BF16),
            pltpu.VMEM((nz, cap2, LANES), BF16),
            pltpu.VMEM((nz, cap2, LANES), BF16),
            pltpu.VMEM((nz, cap2, 2 * LANES), BF16),
            pltpu.VMEM((nz, cap2, 2 * LANES), BF16),
            pltpu.VMEM((n_near, 48, LANES), BF16),
            pltpu.VMEM((n_near, 48, LANES), BF16),
            pltpu.VMEM((120, WIDE + 2 * LANES), F32),
            pltpu.VMEM((120, WIDE + 2 * LANES), F32),
            pltpu.VMEM((80, WIDE), F32),
            pltpu.VMEM((80, WIDE), F32),
            pltpu.VMEM((80, WIDE), BF16),
            pltpu.VMEM((LANES, WIDE), BF16),
            pltpu.VMEM((LANES, 2 * LANES), F32),
            dma((n_near,)),
            dma((n_near,)),
            dma((nz,)),
            dma((nz,)),
            dma((nz,)),
            dma((nz,)),
            dma((n_near,)),
            dma((n_near,)),
            dma((NDYN, 2)),
            dma((NDYN, 2)),
            dma((8,)),
            pltpu.SemaphoreType.REGULAR,
            pltpu.SemaphoreType.REGULAR,
        ],
        compiler_params=pltpu.CompilerParams(
            collective_id=0, has_side_effects=True, vmem_limit_bytes=65000 * 1024
        ),
        name="physics_and_dynamics",
    )(gcm, element_op, neighbours, crm_state, assignment.reshape(1, -1), column_cost.reshape(1, -1))
    vmem_limit = pltpu.CompilerParams(vmem_limit_bytes=65000 * 1024)
    gout, cout = pl.pallas_call(
        hand_over,
        out_shape=(
            jax.ShapeDtypeStruct(gcm.shape, F32),
            jax.ShapeDtypeStruct(crm_state.shape, BF16),
        ),
        in_specs=[hbm] * 2,
        out_specs=(hbm, hbm),
        scratch_shapes=[
            pltpu.VMEM(gcm.shape, F32),
            pltpu.VMEM(crm_state.shape, BF16),
            dma((1 + PARTS,)),
            dma((1 + PARTS,)),
        ],
        compiler_params=vmem_limit,
        name="hand_over",
    )(gout, cout)
    return gout.transpose(1, 0, 2), cout


def solution(mesh):
    n_grp, n_dev = mesh.shape["grp"], mesh.shape["dev"]
    nz = 16 if n_dev % 32 == 0 else n_dev // 4
    nx = n_dev // (2 * nz)
    cap = 2 * ((COLS + n_dev - 1) // n_dev)
    in_specs = (
        P(("grp", "dev"), None, None),
        P(("grp", "dev"), None, None),
        P(("grp", "dev"), None),
        P(("grp", "dev"), None, None),
        P(("grp", "dev")),
        P(("grp", "dev")),
    )
    out_specs = (P(("grp", "dev"), None, None), P(("grp", "dev"), None, None))
    return jax.shard_map(
        functools.partial(body, (n_grp, nx, nz, cap)),
        mesh=mesh,
        in_specs=in_specs,
        out_specs=out_specs,
        check_vma=False,
    )
```
